256 devices in a mesh: dp: 32 (over z, x), tensor: 8 (over y, core).
Axes of the slice: x: 4, y: 4, z: 8, core: 2. Of those that a mesh axis runs over, the one named last changes fastest.
Arguments:
- up_grad: bfloat16 [8192, 14336], P('dp', 'tensor'), may hold values from -6 to 6
- up_error: float32 [8192, 14336], P('dp', 'tensor'), may hold values from -6 to 6
- up_basis: float32 [14336, 64], P('tensor'), may hold values from -0.046875 to 0.046875
- down_grad: bfloat16 [14336, 8192], P('tensor', 'dp'), may hold values from -6 to 6
- down_error: float32 [14336, 8192], P('tensor', 'dp'), may hold values from -6 to 6
- down_basis: float32 [8192, 64], P('dp'), may hold values from -0.0625 to 0.0625
Outputs:
- up_residual: float32 [8192, 14336], P('dp', 'tensor')
- down_residual: float32 [14336, 8192], P('tensor', 'dp')
- up_left: float32 [8192, 64], P('dp')
- up_right: float32 [14336, 64], P('tensor')
- down_left: float32 [14336, 64], P('tensor')
- down_right: float32 [8192, 64], P('dp')
The draws below stay inside these ranges and needn't reach their ends.
All inputs are finite; a program needn't handle non-finite values.
Results may differ from the reference program's by a relative error of at most 0.0003.
Values sent between devices are 32-bit elements; how exact they have to be, the bound alone decides.
A program may use at most 64 MiB of HBM per device.

```python
import jax
import jax.numpy as jnp
from jax import lax

D = 8192
FFW = 14336
RANK = 64


def level_of(rng, shape, cuts, smallest, top_value):
    loudness = 1.0
    for position, shards_of in cuts:
        draws = jax.random.uniform(jax.random.fold_in(jax.random.fold_in(rng, 6), position), (shards_of,), jnp.float32, smallest / len(cuts), top_value / len(cuts))
        loudness = loudness * jnp.repeat(jnp.exp(draws), shape[position] // shards_of).reshape((-1,) + (1,) * (len(shape) - 1 - position))
    return loudness


def noise(key, shape, spread, limit, pieces=(), held_as=jnp.bfloat16):
    gain = level_of(key, shape, pieces, -0.22, 0.18) if pieces else 1.0
    array = jax.random.normal(key, shape, jnp.float32) * spread * gain
    return jnp.minimum(jnp.maximum(array, -limit), limit).astype(held_as)


def setup_inputs(seed: int = 0) -> dict:
    key_of = jax.random.split(jax.random.key(seed), 7)
    return {
        "up_grad": noise(key_of[0], (D, FFW), 1.0, 6.0, ((0, 32), (1, 8))),
        "up_error": noise(key_of[1], (D, FFW), 0.5, 6.0, ((0, 32), (1, 8)), jnp.float32),
        "up_basis": noise(key_of[2], (FFW, RANK), FFW ** -0.5, 0.046875, ((0, 8),), jnp.float32),
        "down_grad": noise(key_of[3], (FFW, D), 1.0, 6.0, ((0, 8), (1, 32))),
        "down_error": noise(key_of[4], (FFW, D), 0.5, 6.0, ((0, 8), (1, 32)), jnp.float32),
        "down_basis": noise(key_of[5], (D, RANK), D ** -0.5, 0.0625, ((0, 32),), jnp.float32),
    }


highest = lax.Precision.HIGHEST

def product(left, right):
    return jnp.dot(left.astype(jnp.float32), right.astype(jnp.float32), precision=highest, preferred_element_type=jnp.float32)

def orthonormal(matrix):
    gram = product(matrix.T, matrix)
    lower = jnp.linalg.cholesky(gram)
    return lax.linalg.triangular_solve(lower, matrix, left_side=False, lower=True, transpose_a=True)

def compress(grad, error, start_basis):
    accum = grad.astype(jnp.float32) + error
    left_sum = product(accum, start_basis)
    left_hat = orthonormal(left_sum)
    right_sum = product(accum.T, left_hat)
    residual = accum - product(left_hat, right_sum.T)
    return (residual, left_hat, right_sum)

def reference(up_grad, up_error, up_basis, down_grad, down_error, down_basis):
    up_res, up_hat, up_fac = compress(up_grad, up_error, up_basis)
    down_res, down_hat, down_fac = compress(down_grad, down_error, down_basis)
    return (up_res, down_res, up_hat, up_fac, down_hat, down_fac)
```

```python
import jax
import jax.numpy as jnp
from jax import lax
from jax.experimental import pallas as pl
from jax.experimental.pallas import tpu as pltpu
from jax.sharding import PartitionSpec as P

MESH = pl.DeviceIdType.MESH
F32 = jnp.float32
BF16 = jnp.bfloat16
BLK = 256
NB = 7
RANK = 64
NZ, NX, NY, NC = 8, 4, 4, 2
SUB = RANK // NX


def split(a):
    hi = a.astype(BF16)
    lo = (a - hi.astype(F32)).astype(BF16)
    return hi, lo


def dot(a, b, dims):
    return lax.dot_general(a, b, (dims, ((), ())), preferred_element_type=F32)


NN = ((1,), (0,))
NT = ((1,), (1,))
TN = ((0,), (0,))


def product3(cat, hi_part, right_hi, right_lo, dims):
    both = dot(cat, right_hi, dims)
    return both[:RANK] + both[RANK:] + dot(hi_part, right_lo, dims)


def gram(cat):
    c = dot(cat, cat, NT)
    return c[:RANK, :RANK] + c[:RANK, RANK:] + c[RANK:, :RANK] + c[RANK:, RANK:]


def pack(g):
    return jnp.concatenate([g[:32], g[32:]], axis=1)


def unpack(p):
    return jnp.concatenate([p[:, :RANK], p[:, RANK:]], axis=0)


def inverse_factor(g):
    sub = lax.broadcasted_iota(jnp.int32, (8, 128), 0)
    lane = lax.broadcasted_iota(jnp.int32, (8, 128), 1)
    groups = []
    for i in range(8):
        eye = (lane[:, :RANK] == sub[:, :RANK] + 8 * i).astype(F32)
        groups.append(jnp.concatenate([eye, g[8 * i : 8 * i + 8]], axis=1))
    scales = [jnp.ones((8, 128), F32) for _ in range(8)]
    for k in range(RANK):
        b, r = k // 8, k % 8
        row = jnp.broadcast_to(groups[b][r : r + 1, :], (8, 128))
        pivot = jnp.broadcast_to(groups[b][r : r + 1, RANK + k : RANK + k + 1], (8, 128))
        scales[b] = jnp.where(sub == r, 1.0 / jnp.sqrt(pivot), scales[b])
        scaled = row * (1.0 / pivot)
        for i in range(b, 8):
            col = jnp.broadcast_to(groups[i][:, RANK + k : RANK + k + 1], (8, 128))
            if i == b:
                col = jnp.where(sub > r, col, 0.0)
            groups[i] = groups[i] - col * scaled
    return jnp.concatenate([groups[i][:, :RANK] * scales[i][:, :RANK] for i in range(8)], axis=0)


def triple_left(a):
    hi, lo = split(a)
    return jnp.concatenate([hi, lo, hi], axis=1)


def triple_right(a):
    hi, lo = split(a)
    return jnp.concatenate([hi, hi, lo], axis=0)


def wait_bytes(ref, sem):
    pltpu.make_async_copy(ref, ref, sem).wait()


def kernel(
    gu, eu, bu, gd, ed, bd,
    ru, rd, lu, wu, ld, wd,
    gub, eub, uh, ul, gdb, edb, dh, dl, bub, bdb,
    src, rx, tx, zrx, out,
    part, crx, half, yb, gpart, gx, gz, gsum, gt,
    sem_load, sem_store, sem_base,
    s_x, s_z, s_ag, r_x, r_z, r_zag, r_xag,
    s_c, r_c, s_y, r_y, s_g, r_g,
):
    dp = lax.axis_index("dp")
    t = lax.axis_index("tensor")
    z, x = dp // NX, dp % NX
    y, c = t // NC, t % NC

    def to_x(d):
        return (z * NX + lax.rem(x + d, NX), t)

    def to_z(target):
        return (target * NX + x, t)

    def to_t(dy, dc):
        return (dp, lax.rem(y + dy, NY) * NC + lax.rem(c + dc, NC))

    others_t = [(dy, dc) for dy in (2, 1, 3, 0) for dc in range(NC) if (dy, dc) != (0, 0)]

    barrier = pltpu.get_barrier_semaphore()
    peers = [to_z(lax.rem(z + d, NZ)) for d in (4, 3, 5, 2, 6, 1, 7)]
    peers += [to_x(d) for d in (2, 1, 3)] + [to_t(*o) for o in others_t]
    for peer in peers:
        pl.semaphore_signal(barrier, inc=1, device_id=peer, device_id_type=MESH)

    skip = (NZ - 1) - z
    at = jnp.where(skip >= 4, 2 * (skip - 4), 2 * (4 - skip) - 1)
    order = []
    for i in range(NB):
        ip = i + jnp.where(i >= at, 1, 0)
        dz = jnp.where(lax.rem(ip, 2) == 1, 4 - (ip + 1) // 2, 4 + ip // 2)
        order.append(lax.rem(z + dz, NZ))
    owner = z < NB
    rows = pl.ds(pl.multiple_of(x * SUB, SUB), SUB)

    def copy_to(a, b, send, recv, device):
        pltpu.make_async_remote_copy(
            src_ref=a, dst_ref=b, send_sem=send, recv_sem=recv, device_id=device, device_id_type=MESH
        ).start()

    base_d = pltpu.make_async_copy(bd, bdb, sem_base.at[0])
    base_d.start()
    loads_d = []
    for i in range(NB):
        cut = pl.ds(pl.multiple_of(order[i] * BLK, BLK), BLK)
        a = pltpu.make_async_copy(gd.at[cut, :], gdb.at[order[i]], sem_load.at[0, i])
        b = pltpu.make_async_copy(ed.at[cut, :], edb.at[order[i]], sem_load.at[1, i])
        a.start()
        b.start()
        loads_d.append((a, b))
    base_u = pltpu.make_async_copy(bu, bub, sem_base.at[1])
    base_u.start()
    loads_u = []
    for j in range(NB):
        cut = pl.ds(j * BLK, BLK)
        a = pltpu.make_async_copy(gu.at[:, cut], gub.at[j], sem_load.at[2, j])
        b = pltpu.make_async_copy(eu.at[:, cut], eub.at[j], sem_load.at[3, j])
        a.start()
        b.start()
        loads_u.append((a, b))

    def x_send(a, i):
        j = order[i]
        for d in (2, 1, 3):
            there = pl.ds(pl.multiple_of(lax.rem(x + d, NX) * SUB, SUB), SUB)
            copy_to(src.at[a, j, there], rx.at[a, i, d - 1], s_x.at[a], r_x.at[a, i], to_x(d))

    def z_send(a, i):
        j = order[i]
        wait_bytes(rx.at[a, i], r_x.at[a, i])
        total = src[a, j, rows, :] + rx[a, i, 0] + rx[a, i, 1] + rx[a, i, 2]
        if i < NB - 1:
            tx[a, i] = total
            copy_to(tx.at[a, i], zrx.at[a, z], s_z.at[a], r_z.at[a], to_z(j))
        else:

            @pl.when(owner)
            def _():
                zrx[a, z] = total

            @pl.when(jnp.logical_not(owner))
            def _():
                tx[a, i] = total
                copy_to(tx.at[a, i], zrx.at[a, z], s_z.at[a], r_z.at[a], to_z(j))

    def reduce_gather(a):
        @pl.when(owner)
        def _():
            wait_bytes(zrx.at[a, pl.ds(0, 7)], r_z.at[a])
            total = zrx[a, 0]
            for s in range(1, NZ):
                total = total + zrx[a, s]
            out[a, z, rows, :] = total
            mine = out.at[a, z, rows]
            for d in (4, 3, 5, 2, 6, 1, 7):
                copy_to(mine, mine, s_ag.at[a], r_zag.at[a, z], to_z(lax.rem(z + d, NZ)))

    def forward(a, i):
        j = order[i]
        block = out.at[a, j, rows]

        def arrive():
            wait_bytes(block, r_zag.at[a, j])

        if i < NB - 1:
            arrive()
        else:
            pl.when(jnp.logical_not(owner))(arrive)
        for d in (2, 1, 3):
            copy_to(block, block, s_ag.at[a], r_xag.at[a, j], to_x(d))

    def gathered(a, i):
        wait_bytes(rx.at[a, 0], r_xag.at[a, order[i]])

    def dp_sends_done(a):
        wait_bytes(rx.at[a], s_x.at[a])
        wait_bytes(rx.at[a], s_ag.at[a])

        @pl.when(owner)
        def _():
            wait_bytes(zrx.at[a, pl.ds(0, 6)], s_z.at[a])
            wait_bytes(zrx.at[a, pl.ds(0, 7)], s_ag.at[a])

        @pl.when(jnp.logical_not(owner))
        def _():
            wait_bytes(zrx.at[a, pl.ds(0, 7)], s_z.at[a])

    def c_send(a):
        copy_to(part.at[a, 1 - c], crx.at[a], s_c.at[a], r_c.at[a], to_t(0, 1))

    def y_send(a):
        wait_bytes(crx.at[a], r_c.at[a])
        total = part[a, c] + crx[a]
        half[a] = total
        yb[a, c * NY + y] = total
        for dy, dc in others_t:
            copy_to(half.at[a], yb.at[a, c * NY + y], s_y.at[a], r_y.at[a], to_t(dy, dc))

    def y_sum(a):
        wait_bytes(yb.at[a, pl.ds(0, 7)], r_y.at[a])
        halves = []
        for h in range(2):
            total = yb[a, h * 4]
            for s in range(1, 4):
                total = total + yb[a, h * 4 + s]
            halves.append(total)
        return jnp.concatenate(halves, axis=0)

    base_d.wait()
    bd_hi, bd_lo = split(bdb[...])
    bd_cat = jnp.concatenate([bd_hi, bd_lo], axis=0)
    for i in range(NB):
        j = order[i]
        loads_d[i][0].wait()
        loads_d[i][1].wait()
        acc = gdb[j].astype(F32) + edb[j]
        edb[j] = acc
        hi, lo = split(acc)
        dh[j] = hi
        dl[j] = lo
        src[0, j] = product3(bd_cat, bd_hi, hi, lo, NT)
    pl.semaphore_wait(barrier, len(peers))
    for i in range(NB):
        x_send(0, i)

    base_u.wait()
    total = jnp.zeros((RANK, BLK), F32)
    for j in range(NB):
        loads_u[j][0].wait()
        loads_u[j][1].wait()
        acc = gub[j].astype(F32) + eub[j]
        eub[j] = acc
        hi, lo = split(acc)
        uh[j] = hi
        ul[j] = lo
        b_hi, b_lo = split(bub[:, j * BLK : (j + 1) * BLK])
        total = total + product3(jnp.concatenate([b_hi, b_lo], axis=0), b_hi, hi, lo, NT)
    part[0, 0] = total[:32]
    part[0, 1] = total[32:]
    c_send(0)
    y_send(0)

    for i in range(NB):
        z_send(0, i)

    xu = y_sum(0)
    xu_hi, xu_lo = split(xu)
    xu_cat = jnp.concatenate([xu_hi, xu_lo], axis=0)
    g = pack(gram(xu_cat))
    gpart[0] = g
    gx[x] = g
    for d in (2, 1, 3):
        copy_to(gpart.at[0], gx.at[x], s_g.at[0], r_g.at[0], to_x(d))
    for i in range(NB):
        j = order[i]
        src[1, j] = product3(xu_cat, xu_hi, uh[j], ul[j], NN)
        x_send(1, i)

    reduce_gather(0)

    wait_bytes(gx.at[pl.ds(0, 3)], r_g.at[0])
    g = gx[0] + gx[1] + gx[2] + gx[3]
    gsum[...] = g
    gz[z] = g
    for d in (4, 3, 5, 2, 6, 1, 7):
        copy_to(gsum, gz.at[z], s_g.at[1], r_g.at[1], to_z(lax.rem(z + d, NZ)))

    for i in reversed(range(NB)):
        forward(0, i)
    for i in range(NB):
        z_send(1, i)

    prod = jnp.zeros((RANK, BLK), F32)
    gsq = jnp.zeros((RANK, RANK), F32)
    for i in reversed(range(NB)):
        gathered(0, i)
    for j in range(NB):
        hi, lo = split(out[0, j])
        cat = jnp.concatenate([hi, lo], axis=0)
        gsq = gsq + gram(cat)
        prod = prod + product3(cat, hi, dh[j], dl[j], NN)
    g = pack(gsq)
    gpart[1] = g
    gt[t] = g
    for dy, dc in others_t:
        copy_to(gpart.at[1], gt.at[t], s_g.at[2], r_g.at[2], to_t(dy, dc))
    part[1, 0] = prod[:32]
    part[1, 1] = prod[32:]
    c_send(1)

    reduce_gather(1)
    y_send(1)

    wait_bytes(gz.at[pl.ds(0, 7)], r_g.at[1])
    g = gz[0]
    for s in range(1, NZ):
        g = g + gz[s]
    inv_u = triple_left(inverse_factor(unpack(g)))
    left_u = dot(inv_u, triple_right(xu), NN)
    lu[...] = left_u
    left_u_t = triple_left(left_u.T)

    for i in reversed(range(NB)):
        forward(1, i)

    wait_bytes(gt.at[pl.ds(0, 7)], r_g.at[2])
    g = gt[0]
    for s in range(1, NY * NC):
        g = g + gt[s]
    inv_d = triple_left(inverse_factor(unpack(g)))
    right_d = dot(inv_d, triple_right(y_sum(1)), NN)
    wd[...] = right_d
    right_d3 = triple_right(right_d)
    stores = []
    for j in range(NB):
        left = dot(inv_d, triple_right(out[0, j]), NN)
        ld[:, j * BLK : (j + 1) * BLK] = left
        edb[j] = edb[j] - dot(triple_left(left.T), right_d3, NN)
        store = pltpu.make_async_copy(edb.at[j], rd.at[pl.ds(j * BLK, BLK), :], sem_store.at[0, j])
        store.start()
        stores.append(store)

    for i in reversed(range(NB)):
        gathered(1, i)
    for j in range(NB):
        right = dot(inv_u, triple_right(out[1, j]), NN)
        wu[:, j * BLK : (j + 1) * BLK] = right
        eub[j] = eub[j] - dot(left_u_t, triple_right(right), NN)
        store = pltpu.make_async_copy(eub.at[j], ru.at[:, pl.ds(j * BLK, BLK)], sem_store.at[1, j])
        store.start()
        stores.append(store)

    dp_sends_done(0)
    dp_sends_done(1)
    for a in range(2):
        wait_bytes(crx.at[a], s_c.at[a])
        wait_bytes(yb.at[a, pl.ds(0, 7)], s_y.at[a])
    wait_bytes(gz.at[pl.ds(0, 3)], s_g.at[0])
    wait_bytes(gz.at[pl.ds(0, 7)], s_g.at[1])
    wait_bytes(gz.at[pl.ds(0, 7)], s_g.at[2])
    for store in stores:
        store.wait()


def on_device(up_grad, up_error, up_basis, down_grad, down_error, down_basis):
    any_space = pl.BlockSpec(memory_space=pl.ANY)
    vmem = pl.BlockSpec(memory_space=pltpu.VMEM)
    dma = pltpu.SemaphoreType.DMA
    wide = NB * BLK
    ru, rd, lu, wu, ld, wd = pl.pallas_call(
        kernel,
        out_shape=(
            jax.ShapeDtypeStruct((BLK, wide), F32),
            jax.ShapeDtypeStruct((wide, BLK), F32),
            jax.ShapeDtypeStruct((RANK, BLK), F32),
            jax.ShapeDtypeStruct((RANK, wide), F32),
            jax.ShapeDtypeStruct((RANK, wide), F32),
            jax.ShapeDtypeStruct((RANK, BLK), F32),
        ),
        in_specs=[any_space] * 6,
        out_specs=(any_space, any_space, vmem, vmem, vmem, vmem),
        scratch_shapes=[
            pltpu.VMEM((NB, BLK, BLK), BF16),
            pltpu.VMEM((NB, BLK, BLK), F32),
            pltpu.VMEM((NB, BLK, BLK), BF16),
            pltpu.VMEM((NB, BLK, BLK), BF16),
            pltpu.VMEM((NB, BLK, BLK), BF16),
            pltpu.VMEM((NB, BLK, BLK), F32),
            pltpu.VMEM((NB, BLK, BLK), BF16),
            pltpu.VMEM((NB, BLK, BLK), BF16),
            pltpu.VMEM((RANK, wide), F32),
            pltpu.VMEM((RANK, BLK), F32),
            pltpu.VMEM((2, NB, RANK, BLK), F32),
            pltpu.VMEM((2, NB, 3, SUB, BLK), F32),
            pltpu.VMEM((2, NB, SUB, BLK), F32),
            pltpu.VMEM((2, NZ, SUB, BLK), F32),
            pltpu.VMEM((2, NB, RANK, BLK), F32),
            pltpu.VMEM((2, 2, RANK // 2, BLK), F32),
            pltpu.VMEM((2, RANK // 2, BLK), F32),
            pltpu.VMEM((2, RANK // 2, BLK), F32),
            pltpu.VMEM((2, 8, RANK // 2, BLK), F32),
            pltpu.VMEM((2, RANK // 2, 128), F32),
            pltpu.VMEM((NX, RANK // 2, 128), F32),
            pltpu.VMEM((NZ, RANK // 2, 128), F32),
            pltpu.VMEM((RANK // 2, 128), F32),
            pltpu.VMEM((NY * NC, RANK // 2, 128), F32),
            dma((4, NB)),
            dma((2, NB)),
            dma((2,)),
            dma((2,)),
            dma((2,)),
            dma((2,)),
            dma((2, NB)),
            dma((2,)),
            dma((2, NB)),
            dma((2, NB)),
            dma((2,)),
            dma((2,)),
            dma((2,)),
            dma((2,)),
            dma((3,)),
            dma((3,)),
        ],
        compiler_params=pltpu.CompilerParams(
            collective_id=0, has_side_effects=True, vmem_limit_bytes=32 * 2**20
        ),
    )(up_grad, up_error, up_basis.T, down_grad, down_error, down_basis.T)
    return ru, rd, lu.T, wu.T, ld.T, wd.T


def solution(mesh):
    placed = (
        P("dp", "tensor"),
        P("dp", "tensor"),
        P("tensor", None),
        P("tensor", "dp"),
        P("tensor", "dp"),
        P("dp", None),
    )
    return jax.shard_map(
        on_device,
        mesh=mesh,
        in_specs=placed,
        out_specs=(
            P("dp", "tensor"),
            P("tensor", "dp"),
            P("dp", None),
            P("tensor", None),
            P("tensor", None),
            P("dp", None),
        ),
        check_vma=False,
    )
```

```python
import jax
import jax.numpy as jnp
from jax import lax
from jax.experimental import pallas as pl
from jax.experimental.pallas import tpu as pltpu
from jax.sharding import PartitionSpec as P

MESH = pl.DeviceIdType.MESH
F32 = jnp.float32
BF16 = jnp.bfloat16
BLK = 256
NB = 7
RANK = 64
NZ, NX, NY, NC = 8, 4, 4, 2
SUB = RANK // NX


def split(a):
    hi = a.astype(BF16)
    lo = (a - hi.astype(F32)).astype(BF16)
    return hi, lo


def dot(a, b, dims):
    return lax.dot_general(a, b, (dims, ((), ())), preferred_element_type=F32)


NN = ((1,), (0,))
NT = ((1,), (1,))
TN = ((0,), (0,))


def product3(cat, hi_part, right_hi, right_lo, dims):
    both = dot(cat, right_hi, dims)
    return both[:RANK] + both[RANK:] + dot(hi_part, right_lo, dims)


def gram(cat):
    c = dot(cat, cat, NT)
    return c[:RANK, :RANK] + c[:RANK, RANK:] + c[RANK:, :RANK] + c[RANK:, RANK:]


def pack(g):
    return jnp.concatenate([g[:32], g[32:]], axis=1)


def unpack(p):
    return jnp.concatenate([p[:, :RANK], p[:, RANK:]], axis=0)


def inverse_factor(g):
    sub = lax.broadcasted_iota(jnp.int32, (8, 128), 0)
    lane = lax.broadcasted_iota(jnp.int32, (8, 128), 1)
    groups = []
    for i in range(8):
        eye = (lane[:, :RANK] == sub[:, :RANK] + 8 * i).astype(F32)
        groups.append(jnp.concatenate([eye, g[8 * i : 8 * i + 8]], axis=1))
    rows = []
    for b in range(8):
        cols = [[jnp.broadcast_to(groups[i][:, RANK + 8*b + j : RANK + 8*b + j + 1], (8, 128)) for i in range(b, 8)] for j in range(8)]
        pivots = jnp.ones((8, 128), F32)
        for r in range(8):
            pivot = jnp.broadcast_to(cols[r][0][r : r + 1, :], (8, 128))
            inv = 1.0 / pivot
            pivots = jnp.where(sub == r, pivot, pivots)
            f = [c * inv for c in cols[r]]
            f[0] = jnp.where(sub > r, f[0], 0.0)
            for j in range(r + 1, 8):
                cj = jnp.broadcast_to(cols[r][0][j : j + 1, :], (8, 128))
                cols[j] = [cols[j][i] - f[i] * cj for i in range(8 - b)]
            row = jnp.broadcast_to(groups[b][r : r + 1, :], (8, 128))
            for i in range(b, 8):
                groups[i] = groups[i] - f[i - b] * row
        rows.append(groups[b][:, :RANK] * (1.0 / jnp.sqrt(pivots))[:, :RANK])
    return jnp.concatenate(rows, axis=0)


def triple_left(a):
    hi, lo = split(a)
    return jnp.concatenate([hi, lo, hi], axis=1)


def triple_right(a):
    hi, lo = split(a)
    return jnp.concatenate([hi, hi, lo], axis=0)


def wait_bytes(ref, sem):
    pltpu.make_async_copy(ref, ref, sem).wait()


def kernel(
    gu, eu, bu, gd, ed, bd,
    ru, rd, lu, wu, ld, wd,
    gub, eub, uh, ul, gdb, edb, dh, dl, bub, bdb,
    src, rx, tx, zrx, out,
    part, crx, half, yb, gpart, gx, gz, gsum, gt,
    sem_load, sem_base,
    s_x, s_z, s_ag, r_x, r_z, r_zag, r_xag,
    s_c, r_c, s_y, r_y, s_g, r_g,
):
    dp = lax.axis_index("dp")
    t = lax.axis_index("tensor")
    z, x = dp // NX, dp % NX
    y, c = t // NC, t % NC

    def to_x(d):
        return (z * NX + lax.rem(x + d, NX), t)

    def to_z(target):
        return (target * NX + x, t)

    def to_t(dy, dc):
        return (dp, lax.rem(y + dy, NY) * NC + lax.rem(c + dc, NC))

    others_t = [(dy, dc) for dy in (2, 1, 3, 0) for dc in range(NC) if (dy, dc) != (0, 0)]

    barrier = pltpu.get_barrier_semaphore()
    peers = [to_z(lax.rem(z + d, NZ)) for d in (4, 3, 5, 2, 6, 1, 7)]
    peers += [to_x(d) for d in (2, 1, 3)] + [to_t(*o) for o in others_t]
    for peer in peers:
        pl.semaphore_signal(barrier, inc=1, device_id=peer, device_id_type=MESH)

    skip = (NZ - 1) - z
    at = jnp.where(skip >= 4, 2 * (skip - 4), 2 * (4 - skip) - 1)
    order = []
    for i in range(NB):
        ip = i + jnp.where(i >= at, 1, 0)
        dz = jnp.where(lax.rem(ip, 2) == 1, 4 - (ip + 1) // 2, 4 + ip // 2)
        order.append(lax.rem(z + dz, NZ))
    owner = z < NB
    rows = pl.ds(pl.multiple_of(x * SUB, SUB), SUB)

    def copy_to(a, b, send, recv, device):
        pltpu.make_async_remote_copy(
            src_ref=a, dst_ref=b, send_sem=send, recv_sem=recv, device_id=device, device_id_type=MESH
        ).start()

    base_d = pltpu.make_async_copy(bd, bdb, sem_base.at[0])
    base_d.start()
    loads_d = []
    for i in range(NB):
        cut = pl.ds(pl.multiple_of(order[i] * BLK, BLK), BLK)
        a = pltpu.make_async_copy(gd.at[cut, :], gdb.at[order[i]], sem_load.at[0, i])
        b = pltpu.make_async_copy(ed.at[cut, :], edb.at[order[i]], sem_load.at[1, i])
        a.start()
        b.start()
        loads_d.append((a, b))
    base_u = pltpu.make_async_copy(bu, bub, sem_base.at[1])
    base_u.start()
    loads_u = []
    for j in range(NB):
        cut = pl.ds(j * BLK, BLK)
        a = pltpu.make_async_copy(gu.at[:, cut], gub.at[j], sem_load.at[2, j])
        b = pltpu.make_async_copy(eu.at[:, cut], eub.at[j], sem_load.at[3, j])
        a.start()
        b.start()
        loads_u.append((a, b))

    def x_send(a, i):
        j = order[i]
        for d in (2, 1, 3):
            there = pl.ds(pl.multiple_of(lax.rem(x + d, NX) * SUB, SUB), SUB)
            copy_to(src.at[a, j, there], rx.at[a, i, d - 1], s_x.at[a], r_x.at[a, i], to_x(d))

    def z_send(a, i):
        j = order[i]
        wait_bytes(rx.at[a, i], r_x.at[a, i])
        total = src[a, j, rows, :] + rx[a, i, 0] + rx[a, i, 1] + rx[a, i, 2]
        if i < NB - 1:
            tx[a, i] = total
            copy_to(tx.at[a, i], zrx.at[a, z], s_z.at[a], r_z.at[a], to_z(j))
        else:

            @pl.when(owner)
            def _():
                zrx[a, z] = total

            @pl.when(jnp.logical_not(owner))
            def _():
                tx[a, i] = total
                copy_to(tx.at[a, i], zrx.at[a, z], s_z.at[a], r_z.at[a], to_z(j))

    def reduce_gather(a):
        @pl.when(owner)
        def _():
            wait_bytes(zrx.at[a, pl.ds(0, 7)], r_z.at[a])
            total = zrx[a, 0]
            for s in range(1, NZ):
                total = total + zrx[a, s]
            out[a, z, rows, :] = total
            mine = out.at[a, z, rows]
            for d in (4, 3, 5, 2, 6, 1, 7):
                copy_to(mine, mine, s_ag.at[a], r_zag.at[a, z], to_z(lax.rem(z + d, NZ)))

    def forward(a, i):
        j = order[i]
        block = out.at[a, j, rows]

        def arrive():
            wait_bytes(block, r_zag.at[a, j])

        if i < NB - 1:
            arrive()
        else:
            pl.when(jnp.logical_not(owner))(arrive)
        for d in (2, 1, 3):
            copy_to(block, block, s_ag.at[a], r_xag.at[a, j], to_x(d))

    def gathered(a, i):
        wait_bytes(rx.at[a, 0], r_xag.at[a, order[i]])

    def dp_sends_done(a):
        wait_bytes(rx.at[a], s_x.at[a])
        wait_bytes(rx.at[a], s_ag.at[a])

        @pl.when(owner)
        def _():
            wait_bytes(zrx.at[a, pl.ds(0, 6)], s_z.at[a])
            wait_bytes(zrx.at[a, pl.ds(0, 7)], s_ag.at[a])

        @pl.when(jnp.logical_not(owner))
        def _():
            wait_bytes(zrx.at[a, pl.ds(0, 7)], s_z.at[a])

    def c_send(a):
        copy_to(part.at[a, 1 - c], crx.at[a], s_c.at[a], r_c.at[a], to_t(0, 1))

    def y_send(a):
        wait_bytes(crx.at[a], r_c.at[a])
        total = part[a, c] + crx[a]
        half[a] = total
        yb[a, c * NY + y] = total
        for dy, dc in others_t:
            copy_to(half.at[a], yb.at[a, c * NY + y], s_y.at[a], r_y.at[a], to_t(dy, dc))

    def y_sum(a):
        wait_bytes(yb.at[a, pl.ds(0, 7)], r_y.at[a])
        halves = []
        for h in range(2):
            total = yb[a, h * 4]
            for s in range(1, 4):
                total = total + yb[a, h * 4 + s]
            halves.append(total)
        return jnp.concatenate(halves, axis=0)

    base_d.wait()
    bd_hi, bd_lo = split(bdb[...])
    bd_cat = jnp.concatenate([bd_hi, bd_lo], axis=0)
    for i in range(NB):
        j = order[i]
        loads_d[i][0].wait()
        loads_d[i][1].wait()
        acc = gdb[j].astype(F32) + edb[j]
        edb[j] = acc
        hi, lo = split(acc)
        dh[j] = hi
        dl[j] = lo
        src[0, j] = product3(bd_cat, bd_hi, hi, lo, NT)
    pl.semaphore_wait(barrier, len(peers))
    for i in range(NB):
        x_send(0, i)

    base_u.wait()
    total = jnp.zeros((RANK, BLK), F32)
    for j in range(NB):
        loads_u[j][0].wait()
        loads_u[j][1].wait()
        acc = gub[j].astype(F32) + eub[j]
        eub[j] = acc
        hi, lo = split(acc)
        uh[j] = hi
        ul[j] = lo
        b_hi, b_lo = split(bub[:, j * BLK : (j + 1) * BLK])
        total = total + product3(jnp.concatenate([b_hi, b_lo], axis=0), b_hi, hi, lo, NT)
    part[0, 0] = total[:32]
    part[0, 1] = total[32:]
    c_send(0)
    y_send(0)

    for i in range(NB):
        z_send(0, i)

    xu = y_sum(0)
    xu_hi, xu_lo = split(xu)
    xu_cat = jnp.concatenate([xu_hi, xu_lo], axis=0)
    g = pack(gram(xu_cat))
    gpart[0] = g
    gx[x] = g
    for d in (2, 1, 3):
        copy_to(gpart.at[0], gx.at[x], s_g.at[0], r_g.at[0], to_x(d))
    for i in range(NB):
        j = order[i]
        src[1, j] = product3(xu_cat, xu_hi, uh[j], ul[j], NN)
        x_send(1, i)

    reduce_gather(0)

    wait_bytes(gx.at[pl.ds(0, 3)], r_g.at[0])
    g = gx[0] + gx[1] + gx[2] + gx[3]
    gsum[...] = g
    gz[z] = g
    for d in (4, 3, 5, 2, 6, 1, 7):
        copy_to(gsum, gz.at[z], s_g.at[1], r_g.at[1], to_z(lax.rem(z + d, NZ)))

    for i in reversed(range(NB)):
        forward(0, i)
    for i in range(NB):
        z_send(1, i)

    prod = jnp.zeros((RANK, BLK), F32)
    gsq = jnp.zeros((RANK, RANK), F32)
    for i in reversed(range(NB)):
        gathered(0, i)
    for j in range(NB):
        hi, lo = split(out[0, j])
        cat = jnp.concatenate([hi, lo], axis=0)
        gsq = gsq + gram(cat)
        prod = prod + product3(cat, hi, dh[j], dl[j], NN)
    g = pack(gsq)
    gpart[1] = g
    gt[t] = g
    for dy, dc in others_t:
        copy_to(gpart.at[1], gt.at[t], s_g.at[2], r_g.at[2], to_t(dy, dc))
    part[1, 0] = prod[:32]
    part[1, 1] = prod[32:]
    c_send(1)

    reduce_gather(1)
    y_send(1)

    wait_bytes(gz.at[pl.ds(0, 7)], r_g.at[1])
    g = gz[0]
    for s in range(1, NZ):
        g = g + gz[s]
    inv_u = triple_left(inverse_factor(unpack(g)))
    left_u = dot(inv_u, triple_right(xu), NN)
    lu[...] = left_u
    left_u_t = triple_left(left_u.T)

    for i in reversed(range(NB)):
        forward(1, i)

    wait_bytes(gt.at[pl.ds(0, 7)], r_g.at[2])
    g = gt[0]
    for s in range(1, NY * NC):
        g = g + gt[s]
    inv_d = triple_left(inverse_factor(unpack(g)))
    right_d = dot(inv_d, triple_right(y_sum(1)), NN)
    wd[...] = right_d
    right_d3 = triple_right(right_d)
    for j in range(NB):
        left = dot(inv_d, triple_right(out[0, j]), NN)
        ld[:, j * BLK : (j + 1) * BLK] = left
        rd[j * BLK : (j + 1) * BLK, :] = edb[j] - dot(triple_left(left.T), right_d3, NN)

    for i in reversed(range(NB)):
        gathered(1, i)
    for j in range(NB):
        right = dot(inv_u, triple_right(out[1, j]), NN)
        wu[:, j * BLK : (j + 1) * BLK] = right
        ru[:, j * BLK : (j + 1) * BLK] = eub[j] - dot(left_u_t, triple_right(right), NN)

    dp_sends_done(0)
    dp_sends_done(1)
    for a in range(2):
        wait_bytes(crx.at[a], s_c.at[a])
        wait_bytes(yb.at[a, pl.ds(0, 7)], s_y.at[a])
    wait_bytes(gz.at[pl.ds(0, 3)], s_g.at[0])
    wait_bytes(gz.at[pl.ds(0, 7)], s_g.at[1])
    wait_bytes(gz.at[pl.ds(0, 7)], s_g.at[2])


def store_kernel(*refs):
    n = len(refs) // 2
    sems = refs[2 * n]
    copies = [pltpu.make_async_copy(refs[i], refs[n + i], sems.at[i]) for i in range(n)]
    for copy in copies:
        copy.start()
    for copy in copies:
        copy.wait()


def store_all(*arrays):
    return pl.pallas_call(
        store_kernel,
        out_shape=tuple(jax.ShapeDtypeStruct(a.shape, a.dtype) for a in arrays),
        in_specs=[pl.BlockSpec(memory_space=pl.ANY)] * len(arrays),
        out_specs=(pl.BlockSpec(memory_space=pltpu.HBM),) * len(arrays),
        scratch_shapes=[pltpu.SemaphoreType.DMA((len(arrays),))],
        compiler_params=pltpu.CompilerParams(vmem_limit_bytes=2**20),
    )(*arrays)


def on_device(up_grad, up_error, up_basis, down_grad, down_error, down_basis):
    arrays = (up_grad, up_error, up_basis.T, down_grad, down_error, down_basis.T)
    hbm = pl.BlockSpec(memory_space=pltpu.HBM)
    vmem = pl.BlockSpec(memory_space=pltpu.VMEM)
    dma = pltpu.SemaphoreType.DMA
    wide = NB * BLK
    ru, rd, lu, wu, ld, wd = pl.pallas_call(
        kernel,
        out_shape=(
            jax.ShapeDtypeStruct((BLK, wide), F32),
            jax.ShapeDtypeStruct((wide, BLK), F32),
            jax.ShapeDtypeStruct((RANK, BLK), F32),
            jax.ShapeDtypeStruct((RANK, wide), F32),
            jax.ShapeDtypeStruct((RANK, wide), F32),
            jax.ShapeDtypeStruct((RANK, BLK), F32),
        ),
        in_specs=[hbm] * 6,
        out_specs=(vmem,) * 6,
        scratch_shapes=[
            pltpu.VMEM((NB, BLK, BLK), BF16),
            pltpu.VMEM((NB, BLK, BLK), F32),
            pltpu.VMEM((NB, BLK, BLK), BF16),
            pltpu.VMEM((NB, BLK, BLK), BF16),
            pltpu.VMEM((NB, BLK, BLK), BF16),
            pltpu.VMEM((NB, BLK, BLK), F32),
            pltpu.VMEM((NB, BLK, BLK), BF16),
            pltpu.VMEM((NB, BLK, BLK), BF16),
            pltpu.VMEM((RANK, wide), F32),
            pltpu.VMEM((RANK, BLK), F32),
            pltpu.VMEM((2, NB, RANK, BLK), F32),
            pltpu.VMEM((2, NB, 3, SUB, BLK), F32),
            pltpu.VMEM((2, NB, SUB, BLK), F32),
            pltpu.VMEM((2, NZ, SUB, BLK), F32),
            pltpu.VMEM((2, NB, RANK, BLK), F32),
            pltpu.VMEM((2, 2, RANK // 2, BLK), F32),
            pltpu.VMEM((2, RANK // 2, BLK), F32),
            pltpu.VMEM((2, RANK // 2, BLK), F32),
            pltpu.VMEM((2, 8, RANK // 2, BLK), F32),
            pltpu.VMEM((2, RANK // 2, 128), F32),
            pltpu.VMEM((NX, RANK // 2, 128), F32),
            pltpu.VMEM((NZ, RANK // 2, 128), F32),
            pltpu.VMEM((RANK // 2, 128), F32),
            pltpu.VMEM((NY * NC, RANK // 2, 128), F32),
            dma((4, NB)),
            dma((2,)),
            dma((2,)),
            dma((2,)),
            dma((2,)),
            dma((2, NB)),
            dma((2,)),
            dma((2, NB)),
            dma((2, NB)),
            dma((2,)),
            dma((2,)),
            dma((2,)),
            dma((2,)),
            dma((3,)),
            dma((3,)),
        ],
        compiler_params=pltpu.CompilerParams(
            collective_id=0, has_side_effects=True, vmem_limit_bytes=32 * 2**20
        ),
    )(*(pltpu.with_memory_space_constraint(a, pltpu.HBM) for a in arrays))
    ru, rd, lu, wu, ld, wd = store_all(ru, rd, lu, wu, ld, wd)
    return ru, rd, lu.T, wu.T, ld.T, wd.T


def solution(mesh):
    placed = (
        P("dp", "tensor"),
        P("dp", "tensor"),
        P("tensor", None),
        P("tensor", "dp"),
        P("tensor", "dp"),
        P("dp", None),
    )
    return jax.shard_map(
        on_device,
        mesh=mesh,
        in_specs=placed,
        out_specs=(
            P("dp", "tensor"),
            P("tensor", "dp"),
            P("dp", None),
            P("tensor", None),
            P("tensor", None),
            P("dp", None),
        ),
        check_vma=False,
    )
```

```python
import jax
import jax.numpy as jnp
from jax import lax
from jax.experimental import pallas as pl
from jax.experimental.pallas import tpu as pltpu
from jax.sharding import PartitionSpec as P

MESH = pl.DeviceIdType.MESH
F32 = jnp.float32
BF16 = jnp.bfloat16
BLK = 256
NB = 7
RANK = 64
NZ, NX, NY, NC = 8, 4, 4, 2
SUB = RANK // NX


def split(a):
    hi = a.astype(BF16)
    lo = (a - hi.astype(F32)).astype(BF16)
    return hi, lo


def dot(a, b, dims):
    return lax.dot_general(a, b, (dims, ((), ())), preferred_element_type=F32)


NN = ((1,), (0,))
NT = ((1,), (1,))
TN = ((0,), (0,))


def product3(cat, hi_part, right_hi, right_lo, dims):
    both = dot(cat, right_hi, dims)
    return both[:RANK] + both[RANK:] + dot(hi_part, right_lo, dims)


def gram(cat):
    c = dot(cat, cat, NT)
    return c[:RANK, :RANK] + c[:RANK, RANK:] + c[RANK:, :RANK] + c[RANK:, RANK:]


def pack(g):
    return jnp.concatenate([g[:32], g[32:]], axis=1)


def unpack(p):
    return jnp.concatenate([p[:, :RANK], p[:, RANK:]], axis=0)


def inverse_factor(g):
    sub = lax.broadcasted_iota(jnp.int32, (8, 128), 0)
    lane = lax.broadcasted_iota(jnp.int32, (8, 128), 1)
    groups = []
    for i in range(8):
        eye = (lane[:, :RANK] == sub[:, :RANK] + 8 * i).astype(F32)
        groups.append(jnp.concatenate([eye, g[8 * i : 8 * i + 8]], axis=1))
    rows = []
    for b in range(8):
        cols = [[jnp.broadcast_to(groups[i][:, RANK + 8*b + j : RANK + 8*b + j + 1], (8, 128)) for i in range(b, 8)] for j in range(8)]
        pivots = jnp.ones((8, 128), F32)
        for r in range(8):
            pivot = jnp.broadcast_to(cols[r][0][r : r + 1, :], (8, 128))
            inv = 1.0 / pivot
            pivots = jnp.where(sub == r, pivot, pivots)
            f = [c * inv for c in cols[r]]
            f[0] = jnp.where(sub > r, f[0], 0.0)
            for j in range(r + 1, 8):
                cj = jnp.broadcast_to(cols[r][0][j : j + 1, :], (8, 128))
                cols[j] = [cols[j][i] - f[i] * cj for i in range(8 - b)]
            row = jnp.broadcast_to(groups[b][r : r + 1, :], (8, 128))
            for i in range(b, 8):
                groups[i] = groups[i] - f[i - b] * row
        rows.append(groups[b][:, :RANK] * (1.0 / jnp.sqrt(pivots))[:, :RANK])
    return jnp.concatenate(rows, axis=0)


def triple_left(a):
    hi, lo = split(a)
    return jnp.concatenate([hi, lo, hi], axis=1)


def triple_right(a):
    hi, lo = split(a)
    return jnp.concatenate([hi, hi, lo], axis=0)


def wait_bytes(ref, sem):
    pltpu.make_async_copy(ref, ref, sem).wait()


def kernel(
    gu, eu, bu, gd, ed, bd,
    rd, lu, ld, wd, eub, w_out, inv_out, left_out,
    gub, uh, ul, gdb, edb, dh, dl, bub, bdb,
    src, rx, tx, zrx, out,
    part, crx, half, yb, gpart, gx, gz, gsum, gt, lt,
    sem_load, sem_base,
    s_x, s_z, s_ag, r_x, r_z, r_zag, r_xag,
    s_c, r_c, s_y, r_y, s_g, r_g,
):
    dp = lax.axis_index("dp")
    t = lax.axis_index("tensor")
    z, x = dp // NX, dp % NX
    y, c = t // NC, t % NC

    def to_x(d):
        return (z * NX + lax.rem(x + d, NX), t)

    def to_z(target):
        return (target * NX + x, t)

    def to_t(dy, dc):
        return (dp, lax.rem(y + dy, NY) * NC + lax.rem(c + dc, NC))

    others_t = [(dy, dc) for dy in (2, 1, 3, 0) for dc in range(NC) if (dy, dc) != (0, 0)]

    barrier = pltpu.get_barrier_semaphore()
    peers = [to_z(lax.rem(z + d, NZ)) for d in (4, 3, 5, 2, 6, 1, 7)]
    peers += [to_x(d) for d in (2, 1, 3)] + [to_t(*o) for o in others_t]
    for peer in peers:
        pl.semaphore_signal(barrier, inc=1, device_id=peer, device_id_type=MESH)

    skip = (NZ - 1) - z
    at = jnp.where(skip >= 4, 2 * (skip - 4), 2 * (4 - skip) - 1)
    order = []
    for i in range(NB):
        ip = i + jnp.where(i >= at, 1, 0)
        dz = jnp.where(lax.rem(ip, 2) == 1, 4 - (ip + 1) // 2, 4 + ip // 2)
        order.append(lax.rem(z + dz, NZ))
    owner = z < NB
    rows = pl.ds(pl.multiple_of(x * SUB, SUB), SUB)

    def copy_to(a, b, send, recv, device):
        pltpu.make_async_remote_copy(
            src_ref=a, dst_ref=b, send_sem=send, recv_sem=recv, device_id=device, device_id_type=MESH
        ).start()

    base_d = pltpu.make_async_copy(bd, bdb, sem_base.at[0])
    base_d.start()
    loads_d = []
    for i in range(NB):
        cut = pl.ds(pl.multiple_of(order[i] * BLK, BLK), BLK)
        a = pltpu.make_async_copy(gd.at[cut, :], gdb.at[order[i]], sem_load.at[0, i])
        b = pltpu.make_async_copy(ed.at[cut, :], edb.at[order[i]], sem_load.at[1, i])
        a.start()
        b.start()
        loads_d.append((a, b))
    base_u = pltpu.make_async_copy(bu, bub, sem_base.at[1])
    base_u.start()
    loads_u = []
    for j in range(NB):
        cut = pl.ds(j * BLK, BLK)
        a = pltpu.make_async_copy(gu.at[:, cut], gub.at[j], sem_load.at[2, j])
        b = pltpu.make_async_copy(eu.at[:, cut], eub.at[j], sem_load.at[3, j])
        a.start()
        b.start()
        loads_u.append((a, b))

    def x_send(a, i):
        j = order[i]
        for d in (2, 1, 3):
            there = pl.ds(pl.multiple_of(lax.rem(x + d, NX) * SUB, SUB), SUB)
            copy_to(src.at[a, j, there], rx.at[a, i, d - 1], s_x.at[a], r_x.at[a, i], to_x(d))

    def z_send(a, i):
        j = order[i]
        wait_bytes(rx.at[a, i], r_x.at[a, i])
        total = src[a, j, rows, :] + rx[a, i, 0] + rx[a, i, 1] + rx[a, i, 2]
        if i < NB - 1:
            tx[a, i] = total
            copy_to(tx.at[a, i], zrx.at[a, z], s_z.at[a], r_z.at[a], to_z(j))
        else:

            @pl.when(owner)
            def _():
                zrx[a, z] = total

            @pl.when(jnp.logical_not(owner))
            def _():
                tx[a, i] = total
                copy_to(tx.at[a, i], zrx.at[a, z], s_z.at[a], r_z.at[a], to_z(j))

    def reduce_gather(a):
        @pl.when(owner)
        def _():
            wait_bytes(zrx.at[a, pl.ds(0, 7)], r_z.at[a])
            total = zrx[a, 0]
            for s in range(1, NZ):
                total = total + zrx[a, s]
            out[a, z, rows, :] = total
            mine = out.at[a, z, rows]
            for d in (4, 3, 5, 2, 6, 1, 7):
                copy_to(mine, mine, s_ag.at[a], r_zag.at[a, z], to_z(lax.rem(z + d, NZ)))

    def forward(a, i):
        j = order[i]
        block = out.at[a, j, rows]

        def arrive():
            wait_bytes(block, r_zag.at[a, j])

        if i < NB - 1:
            arrive()
        else:
            pl.when(jnp.logical_not(owner))(arrive)
        for d in (2, 1, 3):
            copy_to(block, block, s_ag.at[a], r_xag.at[a, j], to_x(d))

    def gathered(a, i):
        wait_bytes(rx.at[a, 0], r_xag.at[a, order[i]])

    def dp_sends_done(a):
        wait_bytes(rx.at[a], s_x.at[a])
        wait_bytes(rx.at[a], s_ag.at[a])

        @pl.when(owner)
        def _():
            wait_bytes(zrx.at[a, pl.ds(0, 6)], s_z.at[a])
            wait_bytes(zrx.at[a, pl.ds(0, 7)], s_ag.at[a])

        @pl.when(jnp.logical_not(owner))
        def _():
            wait_bytes(zrx.at[a, pl.ds(0, 7)], s_z.at[a])

    def c_send(a):
        copy_to(part.at[a, 1 - c], crx.at[a], s_c.at[a], r_c.at[a], to_t(0, 1))

    def y_send(a):
        wait_bytes(crx.at[a], r_c.at[a])
        total = part[a, c] + crx[a]
        half[a] = total
        yb[a, c * NY + y] = total
        for dy, dc in others_t:
            copy_to(half.at[a], yb.at[a, c * NY + y], s_y.at[a], r_y.at[a], to_t(dy, dc))

    def y_sum(a):
        wait_bytes(yb.at[a, pl.ds(0, 7)], r_y.at[a])
        halves = []
        for h in range(2):
            total = yb[a, h * 4]
            for s in range(1, 4):
                total = total + yb[a, h * 4 + s]
            halves.append(total)
        return jnp.concatenate(halves, axis=0)

    keep = {}

    def part_down():
        base_d.wait()
        hi_b, lo_b = split(bdb[...])
        cat = jnp.concatenate([hi_b, lo_b], axis=0)
        for i in range(NB):
            j = order[i]
            loads_d[i][0].wait()
            loads_d[i][1].wait()
            acc = gdb[j].astype(F32) + edb[j]
            edb[j] = acc
            hi, lo = split(acc)
            dh[j] = hi
            dl[j] = lo
            src[0, j] = product3(cat, hi_b, hi, lo, NT)
            x_send(0, i)

    def part_up():
        base_u.wait()
        total = jnp.zeros((RANK, BLK), F32)
        for j in range(NB):
            loads_u[j][0].wait()
            loads_u[j][1].wait()
            acc = gub[j].astype(F32) + eub[j]
            eub[j] = acc
            hi, lo = split(acc)
            uh[j] = hi
            ul[j] = lo
            hi_b, lo_b = split(bub[:, j * BLK : (j + 1) * BLK])
            total = total + product3(jnp.concatenate([hi_b, lo_b], axis=0), hi_b, hi, lo, NT)
        part[0, 0] = total[:32]
        part[0, 1] = total[32:]

    def enter():
        pl.semaphore_wait(barrier, len(peers))

    def z_sends(a):
        for i in range(NB):
            z_send(a, i)

    def gram_up_x():
        xu = y_sum(0)
        keep["xu"] = xu
        hi, lo = split(xu)
        cat = jnp.concatenate([hi, lo], axis=0)
        keep["xu_split"] = (hi, cat)
        g = pack(gram(cat))
        gpart[0] = g
        gx[x] = g
        for d in (2, 1, 3):
            copy_to(gpart.at[0], gx.at[x], s_g.at[0], r_g.at[0], to_x(d))

    def second_up():
        hi, cat = keep["xu_split"]
        for i in range(NB):
            j = order[i]
            src[1, j] = product3(cat, hi, uh[j], ul[j], NN)
            x_send(1, i)

    def gram_up_z():
        wait_bytes(gx.at[pl.ds(0, 3)], r_g.at[0])
        g = gx[0] + gx[1] + gx[2] + gx[3]
        gsum[...] = g
        gz[z] = g
        for d in (4, 3, 5, 2, 6, 1, 7):
            copy_to(gsum, gz.at[z], s_g.at[1], r_g.at[1], to_z(lax.rem(z + d, NZ)))

    def second_down():
        prod = jnp.zeros((RANK, BLK), F32)
        gsq = jnp.zeros((RANK, RANK), F32)
        for i in reversed(range(NB)):
            gathered(0, i)
        for j in range(NB):
            hi, lo = split(out[0, j])
            cat = jnp.concatenate([hi, lo], axis=0)
            gsq = gsq + gram(cat)
            prod = prod + product3(cat, hi, dh[j], dl[j], NN)
        g = pack(gsq)
        gpart[1] = g
        gt[t] = g
        part[1, 0] = prod[:32]
        part[1, 1] = prod[32:]
        c_send(1)
        for dy, dc in others_t:
            copy_to(gpart.at[1], gt.at[t], s_g.at[2], r_g.at[2], to_t(dy, dc))

    def factor_up():
        wait_bytes(gz.at[pl.ds(0, 7)], r_g.at[1])
        g = gz[0]
        for s in range(1, NZ):
            g = g + gz[s]
        keep["inv_u"] = triple_left(inverse_factor(unpack(g)))
        left = dot(keep["inv_u"], triple_right(keep["xu"]), NN)
        lu[...] = left
        keep["left_u"] = triple_left(left.T)

    def factor_down():
        wait_bytes(gt.at[pl.ds(0, 7)], r_g.at[2])
        g = gt[0]
        for s in range(1, NY * NC):
            g = g + gt[s]
        keep["inv_d"] = triple_left(inverse_factor(unpack(g)))

    def left_down():
        for j in range(NB):
            left = dot(keep["inv_d"], triple_right(out[0, j]), NN)
            ld[:, j * BLK : (j + 1) * BLK] = left
            lt[j] = triple_left(left.T)

    def last_down():
        right = dot(keep["inv_d"], triple_right(y_sum(1)), NN)
        wd[...] = right
        right = triple_right(right)
        for j in range(NB):
            rd[j * BLK : (j + 1) * BLK, :] = edb[j] - dot(lt[j], right, NN)

    def tensor_sends_done(a):
        wait_bytes(crx.at[a], s_c.at[a])
        wait_bytes(yb.at[a, pl.ds(0, 7)], s_y.at[a])

    enter()
    part_down()
    part_up()
    c_send(0)
    y_send(0)
    z_sends(0)
    gram_up_x()
    second_up()
    reduce_gather(0)
    gram_up_z()
    for i in (6, 5, 4):
        forward(0, i)
    for i in range(4):
        z_send(1, i)
        forward(0, 3 - i)
    for i in (4, 5, 6):
        z_send(1, i)
    factor_up()
    reduce_gather(1)
    second_down()
    for i in (6, 5):
        forward(1, i)
    y_send(1)
    for i in (4, 3, 2, 1, 0):
        forward(1, i)
    factor_down()
    left_down()
    last_down()
    dp_sends_done(0)
    tensor_sends_done(0)
    wait_bytes(gz.at[pl.ds(0, 3)], s_g.at[0])
    wait_bytes(gz.at[pl.ds(0, 7)], s_g.at[1])
    tensor_sends_done(1)
    wait_bytes(gz.at[pl.ds(0, 7)], s_g.at[2])
    inv_out[...] = keep["inv_u"]
    left_out[...] = keep["left_u"]
    for i in reversed(range(NB)):
        gathered(1, i)
    w_out[...] = out[1]
    dp_sends_done(1)


def store_kernel(rd, lu, ld, wd, acc, w, inv, left, o_ru, o_rd, o_lu, o_wu, o_ld, o_wd, ru, wu, sems, sems_u):
    copies = [
        pltpu.make_async_copy(a, b, sems.at[i])
        for i, (a, b) in enumerate(((rd, o_rd), (ld, o_ld), (lu, o_lu), (wd, o_wd)))
    ]
    for copy in copies:
        copy.start()
    rights = [dot(inv[...], triple_right(w[j]), NN) for j in range(NB)]
    for j in range(NB):
        cut = pl.ds(j * BLK, BLK)
        right = rights[j]
        wu[:, cut] = right
        ru[:, cut] = acc[j] - dot(left[...], triple_right(right), NN)
        copy = pltpu.make_async_copy(ru.at[:, cut], o_ru.at[:, cut], sems_u.at[j])
        copy.start()
        copies.append(copy)
    copy = pltpu.make_async_copy(wu, o_wu, sems.at[4])
    copy.start()
    copies.append(copy)
    for copy in copies:
        copy.wait()


def store_all(*arrays):
    wide = NB * BLK
    vmem = pl.BlockSpec(memory_space=pltpu.VMEM)
    dma = pltpu.SemaphoreType.DMA
    return pl.pallas_call(
        store_kernel,
        out_shape=(
            jax.ShapeDtypeStruct((BLK, wide), F32),
            jax.ShapeDtypeStruct((wide, BLK), F32),
            jax.ShapeDtypeStruct((RANK, BLK), F32),
            jax.ShapeDtypeStruct((RANK, wide), F32),
            jax.ShapeDtypeStruct((RANK, wide), F32),
            jax.ShapeDtypeStruct((RANK, BLK), F32),
        ),
        in_specs=[pl.BlockSpec(memory_space=pl.ANY)] * 4 + [vmem] * 4,
        out_specs=(pl.BlockSpec(memory_space=pltpu.HBM),) * 6,
        scratch_shapes=[
            pltpu.VMEM((BLK, wide), F32),
            pltpu.VMEM((RANK, wide), F32),
            dma((5,)),
            dma((NB,)),
        ],
        compiler_params=pltpu.CompilerParams(vmem_limit_bytes=16 * 2**20),
    )(*arrays)


def on_device(up_grad, up_error, up_basis, down_grad, down_error, down_basis):
    arrays = (up_grad, up_error, up_basis.T, down_grad, down_error, down_basis.T)
    hbm = pl.BlockSpec(memory_space=pltpu.HBM)
    vmem = pl.BlockSpec(memory_space=pltpu.VMEM)
    dma = pltpu.SemaphoreType.DMA
    wide = NB * BLK
    results = pl.pallas_call(
        kernel,
        out_shape=(
            pltpu.VMEM((wide, BLK), F32),
            pltpu.VMEM((RANK, BLK), F32),
            pltpu.VMEM((RANK, wide), F32),
            pltpu.VMEM((RANK, BLK), F32),
            pltpu.VMEM((NB, BLK, BLK), F32),
            pltpu.VMEM((NB, RANK, BLK), F32),
            pltpu.VMEM((RANK, 3 * RANK), BF16),
            pltpu.VMEM((BLK, 3 * RANK), BF16),
        ),
        in_specs=[hbm] * 6,
        out_specs=(vmem,) * 8,
        scratch_shapes=[
            pltpu.VMEM((NB, BLK, BLK), BF16),
            pltpu.VMEM((NB, BLK, BLK), BF16),
            pltpu.VMEM((NB, BLK, BLK), BF16),
            pltpu.VMEM((NB, BLK, BLK), BF16),
            pltpu.VMEM((NB, BLK, BLK), F32),
            pltpu.VMEM((NB, BLK, BLK), BF16),
            pltpu.VMEM((NB, BLK, BLK), BF16),
            pltpu.VMEM((RANK, wide), F32),
            pltpu.VMEM((RANK, BLK), F32),
            pltpu.VMEM((2, NB, RANK, BLK), F32),
            pltpu.VMEM((2, NB, 3, SUB, BLK), F32),
            pltpu.VMEM((2, NB, SUB, BLK), F32),
            pltpu.VMEM((2, NZ, SUB, BLK), F32),
            pltpu.VMEM((2, NB, RANK, BLK), F32),
            pltpu.VMEM((2, 2, RANK // 2, BLK), F32),
            pltpu.VMEM((2, RANK // 2, BLK), F32),
            pltpu.VMEM((2, RANK // 2, BLK), F32),
            pltpu.VMEM((2, 8, RANK // 2, BLK), F32),
            pltpu.VMEM((2, RANK // 2, 128), F32),
            pltpu.VMEM((NX, RANK // 2, 128), F32),
            pltpu.VMEM((NZ, RANK // 2, 128), F32),
            pltpu.VMEM((RANK // 2, 128), F32),
            pltpu.VMEM((NY * NC, RANK // 2, 128), F32),
            pltpu.VMEM((NB, BLK, 3 * RANK), BF16),
            dma((4, NB)),
            dma((2,)),
            dma((2,)),
            dma((2,)),
            dma((2,)),
            dma((2, NB)),
            dma((2,)),
            dma((2, NB)),
            dma((2, NB)),
            dma((2,)),
            dma((2,)),
            dma((2,)),
            dma((2,)),
            dma((3,)),
            dma((3,)),
        ],
        compiler_params=pltpu.CompilerParams(
            collective_id=0, has_side_effects=True, vmem_limit_bytes=32 * 2**20
        ),
    )(*(pltpu.with_memory_space_constraint(a, pltpu.HBM) for a in arrays))
    ru, rd, lu, wu, ld, wd = store_all(*results)
    return ru, rd, lu.T, wu.T, ld.T, wd.T


def solution(mesh):
    placed = (
        P("dp", "tensor"),
        P("dp", "tensor"),
        P("tensor", None),
        P("tensor", "dp"),
        P("tensor", "dp"),
        P("dp", None),
    )
    return jax.shard_map(
        on_device,
        mesh=mesh,
        in_specs=placed,
        out_specs=(
            P("dp", "tensor"),
            P("tensor", "dp"),
            P("dp", None),
            P("tensor", None),
            P("tensor", None),
            P("dp", None),
        ),
        check_vma=False,
    )
```

```python
import jax
import jax.numpy as jnp
from jax import lax
from jax.experimental import pallas as pl
from jax.experimental.pallas import tpu as pltpu
from jax.sharding import PartitionSpec as P

MESH = pl.DeviceIdType.MESH
F32 = jnp.float32
BF16 = jnp.bfloat16
BLK = 256
NB = 7
RANK = 64
NZ, NX, NY, NC = 8, 4, 4, 2
SUB = RANK // NX


def split(a):
    hi = a.astype(BF16)
    lo = (a - hi.astype(F32)).astype(BF16)
    return hi, lo


def dot(a, b, dims):
    return lax.dot_general(a, b, (dims, ((), ())), preferred_element_type=F32)


NN = ((1,), (0,))
NT = ((1,), (1,))
TN = ((0,), (0,))


def product3(cat, hi_part, right_hi, right_lo, dims):
    both = dot(cat, right_hi, dims)
    return both[:RANK] + both[RANK:] + dot(hi_part, right_lo, dims)


def gram(cat):
    c = dot(cat, cat, NT)
    return c[:RANK, :RANK] + c[:RANK, RANK:] + c[RANK:, :RANK] + c[RANK:, RANK:]


def pack(g):
    return jnp.concatenate([g[:32], g[32:]], axis=1)


def unpack(p):
    return jnp.concatenate([p[:, :RANK], p[:, RANK:]], axis=0)


def inverse_factor(g):
    sub = lax.broadcasted_iota(jnp.int32, (8, 128), 0)
    lane = lax.broadcasted_iota(jnp.int32, (8, 128), 1)
    groups = []
    for i in range(8):
        eye = (lane[:, :RANK] == sub[:, :RANK] + 8 * i).astype(F32)
        groups.append(jnp.concatenate([eye, g[8 * i : 8 * i + 8]], axis=1))
    rows = []
    for b in range(8):
        cols = [[jnp.broadcast_to(groups[i][:, RANK + 8*b + j : RANK + 8*b + j + 1], (8, 128)) for i in range(b, 8)] for j in range(8)]
        pivots = jnp.ones((8, 128), F32)
        for r in range(8):
            pivot = jnp.broadcast_to(cols[r][0][r : r + 1, :], (8, 128))
            inv = 1.0 / pivot
            pivots = jnp.where(sub == r, pivot, pivots)
            f = [c * inv for c in cols[r]]
            f[0] = jnp.where(sub > r, f[0], 0.0)
            for j in range(r + 1, 8):
                cj = jnp.broadcast_to(cols[r][0][j : j + 1, :], (8, 128))
                cols[j] = [cols[j][i] - f[i] * cj for i in range(8 - b)]
            row = jnp.broadcast_to(groups[b][r : r + 1, :], (8, 128))
            for i in range(b, 8):
                groups[i] = groups[i] - f[i - b] * row
        rows.append(groups[b][:, :RANK] * (1.0 / jnp.sqrt(pivots))[:, :RANK])
    return jnp.concatenate(rows, axis=0)


def triple_left(a):
    hi, lo = split(a)
    return jnp.concatenate([hi, lo, hi], axis=1)


def triple_right(a):
    hi, lo = split(a)
    return jnp.concatenate([hi, hi, lo], axis=0)


def wait_bytes(ref, sem):
    pltpu.make_async_copy(ref, ref, sem).wait()


def kernel(
    gu, eu, bu, gd, ed, bd,
    rd, lu, ld, wd, eub, w_out, inv_out, left_out,
    gub, uh, ul, gdb, edb, dh, dl, bub, bdb,
    src, rx, tx, zrx, out,
    part, crx, half, yb, gpart, gx, gz, gsum, gt, lt,
    sem_load, sem_base,
    s_x, s_z, s_ag, r_x, r_z, r_zag, r_xag,
    s_c, r_c, s_y, r_y, s_g, r_g,
):
    dp = lax.axis_index("dp")
    t = lax.axis_index("tensor")
    z, x = dp // NX, dp % NX
    y, c = t // NC, t % NC

    def to_x(d):
        return (z * NX + lax.rem(x + d, NX), t)

    def to_z(target):
        return (target * NX + x, t)

    def to_t(dy, dc):
        return (dp, lax.rem(y + dy, NY) * NC + lax.rem(c + dc, NC))

    others_t = [(dy, dc) for dy in (2, 1, 3, 0) for dc in range(NC) if (dy, dc) != (0, 0)]

    barrier = pltpu.get_barrier_semaphore()
    peers = [to_z(lax.rem(z + d, NZ)) for d in (4, 3, 5, 2, 6, 1, 7)]
    peers += [to_x(d) for d in (2, 1, 3)] + [to_t(*o) for o in others_t]
    for peer in peers:
        pl.semaphore_signal(barrier, inc=1, device_id=peer, device_id_type=MESH)

    skip = (NZ - 1) - z
    at = jnp.where(skip >= 4, 2 * (skip - 4), 2 * (4 - skip) - 1)
    order = []
    for i in range(NB):
        ip = i + jnp.where(i >= at, 1, 0)
        dz = jnp.where(lax.rem(ip, 2) == 1, 4 - (ip + 1) // 2, 4 + ip // 2)
        order.append(lax.rem(z + dz, NZ))
    owner = z < NB
    rows = pl.ds(pl.multiple_of(x * SUB, SUB), SUB)

    def copy_to(a, b, send, recv, device):
        pltpu.make_async_remote_copy(
            src_ref=a, dst_ref=b, send_sem=send, recv_sem=recv, device_id=device, device_id_type=MESH
        ).start()

    base_d = pltpu.make_async_copy(bd, bdb, sem_base.at[0])
    base_d.start()
    loads_d = []
    for i in range(NB):
        cut = pl.ds(pl.multiple_of(order[i] * BLK, BLK), BLK)
        a = pltpu.make_async_copy(gd.at[cut, :], gdb.at[order[i]], sem_load.at[0, i])
        b = pltpu.make_async_copy(ed.at[cut, :], edb.at[order[i]], sem_load.at[1, i])
        a.start()
        b.start()
        loads_d.append((a, b))
    base_u = pltpu.make_async_copy(bu, bub, sem_base.at[1])
    base_u.start()
    loads_u = []
    for j in range(NB):
        cut = pl.ds(j * BLK, BLK)
        a = pltpu.make_async_copy(gu.at[:, cut], gub.at[j], sem_load.at[2, j])
        b = pltpu.make_async_copy(eu.at[:, cut], eub.at[j], sem_load.at[3, j])
        a.start()
        b.start()
        loads_u.append((a, b))

    def x_send(a, i):
        j = order[i]
        for d in (2, 1, 3):
            there = pl.ds(pl.multiple_of(lax.rem(x + d, NX) * SUB, SUB), SUB)
            copy_to(src.at[a, j, there], rx.at[a, i, d - 1], s_x.at[a], r_x.at[a, i], to_x(d))

    def z_send(a, i):
        j = order[i]
        wait_bytes(rx.at[a, i], r_x.at[a, i])
        total = src[a, j, rows, :] + rx[a, i, 0] + rx[a, i, 1] + rx[a, i, 2]
        if i < NB - 1:
            tx[a, i] = total
            copy_to(tx.at[a, i], zrx.at[a, z], s_z.at[a], r_z.at[a], to_z(j))
        else:

            @pl.when(owner)
            def _():
                zrx[a, z] = total

            @pl.when(jnp.logical_not(owner))
            def _():
                tx[a, i] = total
                copy_to(tx.at[a, i], zrx.at[a, z], s_z.at[a], r_z.at[a], to_z(j))

    def reduce_gather(a):
        @pl.when(owner)
        def _():
            wait_bytes(zrx.at[a, pl.ds(0, 7)], r_z.at[a])
            total = zrx[a, 0]
            for s in range(1, NZ):
                total = total + zrx[a, s]
            out[a, z, rows, :] = total
            mine = out.at[a, z, rows]
            for d in (4, 3, 5, 2, 6, 1, 7):
                copy_to(mine, mine, s_ag.at[a], r_zag.at[a, z], to_z(lax.rem(z + d, NZ)))

    def forward(a, i):
        j = order[i]
        block = out.at[a, j, rows]

        def arrive():
            wait_bytes(block, r_zag.at[a, j])

        if i < NB - 1:
            arrive()
        else:
            pl.when(jnp.logical_not(owner))(arrive)
        for d in (2, 1, 3):
            copy_to(block, block, s_ag.at[a], r_xag.at[a, j], to_x(d))

    def gathered(a, i):
        wait_bytes(rx.at[a, 0], r_xag.at[a, order[i]])

    def dp_sends_done(a):
        wait_bytes(rx.at[a], s_x.at[a])
        wait_bytes(rx.at[a], s_ag.at[a])

        @pl.when(owner)
        def _():
            wait_bytes(zrx.at[a, pl.ds(0, 6)], s_z.at[a])
            wait_bytes(zrx.at[a, pl.ds(0, 7)], s_ag.at[a])

        @pl.when(jnp.logical_not(owner))
        def _():
            wait_bytes(zrx.at[a, pl.ds(0, 7)], s_z.at[a])

    def c_send(a):
        copy_to(part.at[a, 1 - c], crx.at[a], s_c.at[a], r_c.at[a], to_t(0, 1))

    def y_send(a):
        wait_bytes(crx.at[a], r_c.at[a])
        total = part[a, c] + crx[a]
        half[a] = total
        yb[a, c * NY + y] = total
        for dy, dc in others_t:
            copy_to(half.at[a], yb.at[a, c * NY + y], s_y.at[a], r_y.at[a], to_t(dy, dc))

    def y_sum(a):
        wait_bytes(yb.at[a, pl.ds(0, 7)], r_y.at[a])
        halves = []
        for h in range(2):
            total = yb[a, h * 4]
            for s in range(1, 4):
                total = total + yb[a, h * 4 + s]
            halves.append(total)
        return jnp.concatenate(halves, axis=0)

    keep = {}

    def base_down():
        base_d.wait()
        hi_b, lo_b = split(bdb[...])
        keep["bd"] = (hi_b, jnp.concatenate([hi_b, lo_b], axis=0))

    def part_down(steps):
        hi_b, cat = keep["bd"]
        for i in steps:
            j = order[i]
            loads_d[i][0].wait()
            loads_d[i][1].wait()
            acc = gdb[j].astype(F32) + edb[j]
            edb[j] = acc
            hi, lo = split(acc)
            dh[j] = hi
            dl[j] = lo
            src[0, j] = product3(cat, hi_b, hi, lo, NT)
            x_send(0, i)

    def part_up():
        base_u.wait()
        total = jnp.zeros((RANK, BLK), F32)
        for j in range(NB):
            loads_u[j][0].wait()
            loads_u[j][1].wait()
            acc = gub[j].astype(F32) + eub[j]
            eub[j] = acc
            hi, lo = split(acc)
            uh[j] = hi
            ul[j] = lo
            hi_b, lo_b = split(bub[:, j * BLK : (j + 1) * BLK])
            total = total + product3(jnp.concatenate([hi_b, lo_b], axis=0), hi_b, hi, lo, NT)
        part[0, 0] = total[:32]
        part[0, 1] = total[32:]

    def enter():
        pl.semaphore_wait(barrier, len(peers))

    def z_sends(a):
        for i in range(NB):
            z_send(a, i)

    def gram_up_x():
        xu = y_sum(0)
        keep["xu"] = xu
        hi, lo = split(xu)
        cat = jnp.concatenate([hi, lo], axis=0)
        keep["xu_split"] = (hi, cat)
        g = pack(gram(cat))
        gpart[0] = g
        gx[x] = g
        for d in (2, 1, 3):
            copy_to(gpart.at[0], gx.at[x], s_g.at[0], r_g.at[0], to_x(d))

    def second_up():
        hi, cat = keep["xu_split"]
        for i in range(NB):
            j = order[i]
            src[1, j] = product3(cat, hi, uh[j], ul[j], NN)
            x_send(1, i)

    def gram_up_z():
        wait_bytes(gx.at[pl.ds(0, 3)], r_g.at[0])
        g = gx[0] + gx[1] + gx[2] + gx[3]
        gsum[...] = g
        gz[z] = g
        for d in (4, 3, 5, 2, 6, 1, 7):
            copy_to(gsum, gz.at[z], s_g.at[1], r_g.at[1], to_z(lax.rem(z + d, NZ)))

    def second_down():
        prod = jnp.zeros((RANK, BLK), F32)
        gsq = jnp.zeros((RANK, RANK), F32)
        for i in reversed(range(NB)):
            gathered(0, i)
        for j in range(NB):
            hi, lo = split(out[0, j])
            cat = jnp.concatenate([hi, lo], axis=0)
            gsq = gsq + gram(cat)
            prod = prod + product3(cat, hi, dh[j], dl[j], NN)
        g = pack(gsq)
        gpart[1] = g
        gt[t] = g
        part[1, 0] = prod[:32]
        part[1, 1] = prod[32:]
        c_send(1)
        for dy, dc in others_t:
            copy_to(gpart.at[1], gt.at[t], s_g.at[2], r_g.at[2], to_t(dy, dc))

    def factor_up():
        wait_bytes(gz.at[pl.ds(0, 7)], r_g.at[1])
        g = gz[0]
        for s in range(1, NZ):
            g = g + gz[s]
        keep["inv_u"] = triple_left(inverse_factor(unpack(g)))
        left = dot(keep["inv_u"], triple_right(keep["xu"]), NN)
        lu[...] = left
        keep["left_u"] = triple_left(left.T)

    def factor_down():
        wait_bytes(gt.at[pl.ds(0, 7)], r_g.at[2])
        g = gt[0]
        for s in range(1, NY * NC):
            g = g + gt[s]
        keep["inv_d"] = triple_left(inverse_factor(unpack(g)))

    def left_down():
        for j in range(NB):
            left = dot(keep["inv_d"], triple_right(out[0, j]), NN)
            ld[:, j * BLK : (j + 1) * BLK] = left
            lt[j] = triple_left(left.T)

    def last_down():
        right = dot(keep["inv_d"], triple_right(y_sum(1)), NN)
        wd[...] = right
        right = triple_right(right)
        for j in range(NB):
            rd[j * BLK : (j + 1) * BLK, :] = edb[j] - dot(lt[j], right, NN)

    def tensor_sends_done(a):
        wait_bytes(crx.at[a], s_c.at[a])
        wait_bytes(yb.at[a, pl.ds(0, 7)], s_y.at[a])

    enter()
    base_down()
    part_down((0, 1))
    part_up()
    c_send(0)
    part_down((2, 3, 4))
    y_send(0)
    part_down((5, 6))
    z_sends(0)
    gram_up_x()
    second_up()
    reduce_gather(0)
    gram_up_z()
    for i in (6, 5, 4):
        forward(0, i)
    for i in range(4):
        z_send(1, i)
        forward(0, 3 - i)
    for i in (4, 5, 6):
        z_send(1, i)
    factor_up()
    reduce_gather(1)
    second_down()
    for i in (6, 5):
        forward(1, i)
    y_send(1)
    for i in (4, 3, 2, 1, 0):
        forward(1, i)
    factor_down()
    left_down()
    last_down()
    dp_sends_done(0)
    tensor_sends_done(0)
    wait_bytes(gz.at[pl.ds(0, 3)], s_g.at[0])
    wait_bytes(gz.at[pl.ds(0, 7)], s_g.at[1])
    tensor_sends_done(1)
    wait_bytes(gz.at[pl.ds(0, 7)], s_g.at[2])
    inv_out[...] = keep["inv_u"]
    left_out[...] = keep["left_u"]
    for i in reversed(range(NB)):
        gathered(1, i)
    w_out[...] = out[1]
    dp_sends_done(1)


def store_kernel(rd, lu, ld, wd, acc, w, inv, left, o_ru, o_rd, o_lu, o_wu, o_ld, o_wd, ru, wu, sems, sems_u):
    copies = [
        pltpu.make_async_copy(a, b, sems.at[i])
        for i, (a, b) in enumerate(((rd, o_rd), (ld, o_ld), (lu, o_lu), (wd, o_wd)))
    ]
    for copy in copies:
        copy.start()
    rights = [dot(inv[...], triple_right(w[j]), NN) for j in range(NB)]
    for j in range(NB):
        cut = pl.ds(j * BLK, BLK)
        right = rights[j]
        wu[:, cut] = right
        ru[:, cut] = acc[j] - dot(left[...], triple_right(right), NN)
        copy = pltpu.make_async_copy(ru.at[:, cut], o_ru.at[:, cut], sems_u.at[j])
        copy.start()
        copies.append(copy)
    copy = pltpu.make_async_copy(wu, o_wu, sems.at[4])
    copy.start()
    copies.append(copy)
    for copy in copies:
        copy.wait()


def store_all(*arrays):
    wide = NB * BLK
    vmem = pl.BlockSpec(memory_space=pltpu.VMEM)
    dma = pltpu.SemaphoreType.DMA
    return pl.pallas_call(
        store_kernel,
        out_shape=(
            jax.ShapeDtypeStruct((BLK, wide), F32),
            jax.ShapeDtypeStruct((wide, BLK), F32),
            jax.ShapeDtypeStruct((RANK, BLK), F32),
            jax.ShapeDtypeStruct((RANK, wide), F32),
            jax.ShapeDtypeStruct((RANK, wide), F32),
            jax.ShapeDtypeStruct((RANK, BLK), F32),
        ),
        in_specs=[pl.BlockSpec(memory_space=pl.ANY)] * 4 + [vmem] * 4,
        out_specs=(pl.BlockSpec(memory_space=pltpu.HBM),) * 6,
        scratch_shapes=[
            pltpu.VMEM((BLK, wide), F32),
            pltpu.VMEM((RANK, wide), F32),
            dma((5,)),
            dma((NB,)),
        ],
        compiler_params=pltpu.CompilerParams(vmem_limit_bytes=16 * 2**20),
    )(*arrays)


def on_device(up_grad, up_error, up_basis, down_grad, down_error, down_basis):
    arrays = (up_grad, up_error, up_basis.T, down_grad, down_error, down_basis.T)
    hbm = pl.BlockSpec(memory_space=pltpu.HBM)
    vmem = pl.BlockSpec(memory_space=pltpu.VMEM)
    dma = pltpu.SemaphoreType.DMA
    wide = NB * BLK
    results = pl.pallas_call(
        kernel,
        out_shape=(
            pltpu.VMEM((wide, BLK), F32),
            pltpu.VMEM((RANK, BLK), F32),
            pltpu.VMEM((RANK, wide), F32),
            pltpu.VMEM((RANK, BLK), F32),
            pltpu.VMEM((NB, BLK, BLK), F32),
            pltpu.VMEM((NB, RANK, BLK), F32),
            pltpu.VMEM((RANK, 3 * RANK), BF16),
            pltpu.VMEM((BLK, 3 * RANK), BF16),
        ),
        in_specs=[hbm] * 6,
        out_specs=(vmem,) * 8,
        scratch_shapes=[
            pltpu.VMEM((NB, BLK, BLK), BF16),
            pltpu.VMEM((NB, BLK, BLK), BF16),
            pltpu.VMEM((NB, BLK, BLK), BF16),
            pltpu.VMEM((NB, BLK, BLK), BF16),
            pltpu.VMEM((NB, BLK, BLK), F32),
            pltpu.VMEM((NB, BLK, BLK), BF16),
            pltpu.VMEM((NB, BLK, BLK), BF16),
            pltpu.VMEM((RANK, wide), F32),
            pltpu.VMEM((RANK, BLK), F32),
            pltpu.VMEM((2, NB, RANK, BLK), F32),
            pltpu.VMEM((2, NB, 3, SUB, BLK), F32),
            pltpu.VMEM((2, NB, SUB, BLK), F32),
            pltpu.VMEM((2, NZ, SUB, BLK), F32),
            pltpu.VMEM((2, NB, RANK, BLK), F32),
            pltpu.VMEM((2, 2, RANK // 2, BLK), F32),
            pltpu.VMEM((2, RANK // 2, BLK), F32),
            pltpu.VMEM((2, RANK // 2, BLK), F32),
            pltpu.VMEM((2, 8, RANK // 2, BLK), F32),
            pltpu.VMEM((2, RANK // 2, 128), F32),
            pltpu.VMEM((NX, RANK // 2, 128), F32),
            pltpu.VMEM((NZ, RANK // 2, 128), F32),
            pltpu.VMEM((RANK // 2, 128), F32),
            pltpu.VMEM((NY * NC, RANK // 2, 128), F32),
            pltpu.VMEM((NB, BLK, 3 * RANK), BF16),
            dma((4, NB)),
            dma((2,)),
            dma((2,)),
            dma((2,)),
            dma((2,)),
            dma((2, NB)),
            dma((2,)),
            dma((2, NB)),
            dma((2, NB)),
            dma((2,)),
            dma((2,)),
            dma((2,)),
            dma((2,)),
            dma((3,)),
            dma((3,)),
        ],
        compiler_params=pltpu.CompilerParams(
            collective_id=0, has_side_effects=True, vmem_limit_bytes=32 * 2**20
        ),
    )(*(pltpu.with_memory_space_constraint(a, pltpu.HBM) for a in arrays))
    ru, rd, lu, wu, ld, wd = store_all(*results)
    return ru, rd, lu.T, wu.T, ld.T, wd.T


def solution(mesh):
    placed = (
        P("dp", "tensor"),
        P("dp", "tensor"),
        P("tensor", None),
        P("tensor", "dp"),
        P("tensor", "dp"),
        P("dp", None),
    )
    return jax.shard_map(
        on_device,
        mesh=mesh,
        in_specs=placed,
        out_specs=(
            P("dp", "tensor"),
            P("tensor", "dp"),
            P("dp", None),
            P("tensor", None),
            P("tensor", None),
            P("dp", None),
        ),
        check_vma=False,
    )
```

```python
import jax
import jax.numpy as jnp
from jax import lax
from jax.experimental import pallas as pl
from jax.experimental.pallas import tpu as pltpu
from jax.sharding import PartitionSpec as P

MESH = pl.DeviceIdType.MESH
F32 = jnp.float32
BF16 = jnp.bfloat16
BLK = 256
NB = 7
RANK = 64
NZ, NX, NY, NC = 8, 4, 4, 2
SUB = RANK // NX


def split(a):
    hi = a.astype(BF16)
    lo = (a - hi.astype(F32)).astype(BF16)
    return hi, lo


def dot(a, b, dims):
    return lax.dot_general(a, b, (dims, ((), ())), preferred_element_type=F32)


NN = ((1,), (0,))
NT = ((1,), (1,))
TN = ((0,), (0,))


def product3(cat, hi_part, right_hi, right_lo, dims):
    both = dot(cat, right_hi, dims)
    return both[:RANK] + both[RANK:] + dot(hi_part, right_lo, dims)


def gram(cat):
    c = dot(cat, cat, NT)
    return c[:RANK, :RANK] + c[:RANK, RANK:] + c[RANK:, :RANK] + c[RANK:, RANK:]


def pack(g):
    return jnp.concatenate([g[:32], g[32:]], axis=1)


def unpack(p):
    return jnp.concatenate([p[:, :RANK], p[:, RANK:]], axis=0)


def inverse_factor(g):
    sub = lax.broadcasted_iota(jnp.int32, (8, 128), 0)
    lane = lax.broadcasted_iota(jnp.int32, (8, 128), 1)
    groups = []
    for i in range(8):
        eye = (lane[:, :RANK] == sub[:, :RANK] + 8 * i).astype(F32)
        groups.append(jnp.concatenate([eye, g[8 * i : 8 * i + 8]], axis=1))
    rows = []
    for b in range(8):
        cols = [[jnp.broadcast_to(groups[i][:, RANK + 8*b + j : RANK + 8*b + j + 1], (8, 128)) for i in range(b, 8)] for j in range(8)]
        pivots = jnp.ones((8, 128), F32)
        for r in range(8):
            pivot = jnp.broadcast_to(cols[r][0][r : r + 1, :], (8, 128))
            inv = 1.0 / pivot
            pivots = jnp.where(sub == r, pivot, pivots)
            f = [c * inv for c in cols[r]]
            f[0] = jnp.where(sub > r, f[0], 0.0)
            for j in range(r + 1, 8):
                cj = jnp.broadcast_to(cols[r][0][j : j + 1, :], (8, 128))
                cols[j] = [cols[j][i] - f[i] * cj for i in range(8 - b)]
            row = jnp.broadcast_to(groups[b][r : r + 1, :], (8, 128))
            for i in range(b, 8):
                groups[i] = groups[i] - f[i - b] * row
        rows.append(groups[b][:, :RANK] * (1.0 / jnp.sqrt(pivots))[:, :RANK])
    return jnp.concatenate(rows, axis=0)


def triple_left(a):
    hi, lo = split(a)
    return jnp.concatenate([hi, lo, hi], axis=1)


def triple_right(a):
    hi, lo = split(a)
    return jnp.concatenate([hi, hi, lo], axis=0)


def wait_bytes(ref, sem):
    pltpu.make_async_copy(ref, ref, sem).wait()


def kernel(
    gu, eu, bu, gd, ed, bd,
    rd, lu, ld, wd, eub, w_out, inv_out, left_out,
    gub, uh, ul, gdb, edb, dh, dl, bub, bdb,
    src, rx, tx, zrx, out,
    part, crx, half, yb, gpart, gx, gz, gsum, gt, lt,
    sem_load, sem_base,
    s_x, s_z, s_ag, r_x, r_z, r_zag, r_xag,
    s_c, r_c, s_y, r_y, s_g, r_g,
):
    dp = lax.axis_index("dp")
    t = lax.axis_index("tensor")
    z, x = dp // NX, dp % NX
    y, c = t // NC, t % NC

    def to_x(d):
        return (z * NX + lax.rem(x + d, NX), t)

    def to_z(target):
        return (target * NX + x, t)

    def to_t(dy, dc):
        return (dp, lax.rem(y + dy, NY) * NC + lax.rem(c + dc, NC))

    others_t = [(dy, dc) for dy in (2, 1, 3, 0) for dc in range(NC) if (dy, dc) != (0, 0)]

    barrier = pltpu.get_barrier_semaphore()
    peers = [to_z(lax.rem(z + d, NZ)) for d in (4, 3, 5, 2, 6, 1, 7)]
    peers += [to_x(d) for d in (2, 1, 3)] + [to_t(*o) for o in others_t]
    for peer in peers:
        pl.semaphore_signal(barrier, inc=1, device_id=peer, device_id_type=MESH)

    skip = (NZ - 1) - z
    at = jnp.where(skip >= 4, 2 * (skip - 4), 2 * (4 - skip) - 1)
    order = []
    for i in range(NB):
        ip = i + jnp.where(i >= at, 1, 0)
        dz = jnp.where(lax.rem(ip, 2) == 1, 4 - (ip + 1) // 2, 4 + ip // 2)
        order.append(lax.rem(z + dz, NZ))
    owner = z < NB
    rows = pl.ds(pl.multiple_of(x * SUB, SUB), SUB)

    def copy_to(a, b, send, recv, device):
        pltpu.make_async_remote_copy(
            src_ref=a, dst_ref=b, send_sem=send, recv_sem=recv, device_id=device, device_id_type=MESH
        ).start()

    base_d = pltpu.make_async_copy(bd, bdb, sem_base.at[0])
    base_d.start()
    loads_d = {}

    def load_down(i):
        cut = pl.ds(pl.multiple_of(order[i] * BLK, BLK), BLK)
        a = pltpu.make_async_copy(gd.at[cut, :], gdb.at[order[i]], sem_load.at[0, i])
        b = pltpu.make_async_copy(ed.at[cut, :], edb.at[order[i]], sem_load.at[1, i])
        a.start()
        b.start()
        loads_d[i] = (a, b)

    for i in range(2):
        load_down(i)
    base_u = pltpu.make_async_copy(bu, bub, sem_base.at[1])
    base_u.start()
    loads_u = []
    for j in range(NB):
        cut = pl.ds(j * BLK, BLK)
        a = pltpu.make_async_copy(gu.at[:, cut], gub.at[j], sem_load.at[2, j])
        b = pltpu.make_async_copy(eu.at[:, cut], eub.at[j], sem_load.at[3, j])
        a.start()
        b.start()
        loads_u.append((a, b))
    for i in range(2, NB):
        load_down(i)

    def x_send(a, i):
        j = order[i]
        for d in (2, 1, 3):
            there = pl.ds(pl.multiple_of(lax.rem(x + d, NX) * SUB, SUB), SUB)
            copy_to(src.at[a, j, there], rx.at[a, i, d - 1], s_x.at[a], r_x.at[a, i], to_x(d))

    def z_send(a, i):
        j = order[i]
        wait_bytes(rx.at[a, i], r_x.at[a, i])
        total = src[a, j, rows, :] + rx[a, i, 0] + rx[a, i, 1] + rx[a, i, 2]
        if i < NB - 1:
            tx[a, i] = total
            copy_to(tx.at[a, i], zrx.at[a, z], s_z.at[a], r_z.at[a], to_z(j))
        else:

            @pl.when(owner)
            def _():
                zrx[a, z] = total

            @pl.when(jnp.logical_not(owner))
            def _():
                tx[a, i] = total
                copy_to(tx.at[a, i], zrx.at[a, z], s_z.at[a], r_z.at[a], to_z(j))

    def reduce_gather(a):
        @pl.when(owner)
        def _():
            wait_bytes(zrx.at[a, pl.ds(0, 7)], r_z.at[a])
            total = zrx[a, 0]
            for s in range(1, NZ):
                total = total + zrx[a, s]
            out[a, z, rows, :] = total
            mine = out.at[a, z, rows]
            for d in (4, 3, 5, 2, 6, 1, 7):
                copy_to(mine, mine, s_ag.at[a], r_zag.at[a, z], to_z(lax.rem(z + d, NZ)))

    def forward(a, i):
        j = order[i]
        block = out.at[a, j, rows]

        def arrive():
            wait_bytes(block, r_zag.at[a, j])

        if i < NB - 1:
            arrive()
        else:
            pl.when(jnp.logical_not(owner))(arrive)
        for d in (2, 1, 3):
            copy_to(block, block, s_ag.at[a], r_xag.at[a, j], to_x(d))

    def gathered(a, i):
        wait_bytes(rx.at[a, 0], r_xag.at[a, order[i]])

    def dp_sends_done(a):
        wait_bytes(rx.at[a], s_x.at[a])
        wait_bytes(rx.at[a], s_ag.at[a])

        @pl.when(owner)
        def _():
            wait_bytes(zrx.at[a, pl.ds(0, 6)], s_z.at[a])
            wait_bytes(zrx.at[a, pl.ds(0, 7)], s_ag.at[a])

        @pl.when(jnp.logical_not(owner))
        def _():
            wait_bytes(zrx.at[a, pl.ds(0, 7)], s_z.at[a])

    def c_send(a):
        copy_to(part.at[a, 1 - c], crx.at[a], s_c.at[a], r_c.at[a], to_t(0, 1))

    def y_send(a):
        wait_bytes(crx.at[a], r_c.at[a])
        total = part[a, c] + crx[a]
        half[a] = total
        yb[a, c * NY + y] = total
        for dy, dc in others_t:
            copy_to(half.at[a], yb.at[a, c * NY + y], s_y.at[a], r_y.at[a], to_t(dy, dc))

    def y_sum(a):
        wait_bytes(yb.at[a, pl.ds(0, 7)], r_y.at[a])
        halves = []
        for h in range(2):
            total = yb[a, h * 4]
            for s in range(1, 4):
                total = total + yb[a, h * 4 + s]
            halves.append(total)
        return jnp.concatenate(halves, axis=0)

    keep = {}

    def base_down():
        base_d.wait()
        hi_b, lo_b = split(bdb[...])
        keep["bd"] = (hi_b, jnp.concatenate([hi_b, lo_b], axis=0))

    def part_down(steps):
        hi_b, cat = keep["bd"]
        for i in steps:
            j = order[i]
            loads_d[i][0].wait()
            loads_d[i][1].wait()
            acc = gdb[j].astype(F32) + edb[j]
            edb[j] = acc
            hi, lo = split(acc)
            dh[j] = hi
            dl[j] = lo
            src[0, j] = product3(cat, hi_b, hi, lo, NT)
            x_send(0, i)

    def part_up():
        base_u.wait()
        total = jnp.zeros((RANK, BLK), F32)
        for j in range(NB):
            loads_u[j][0].wait()
            loads_u[j][1].wait()
            acc = gub[j].astype(F32) + eub[j]
            eub[j] = acc
            hi, lo = split(acc)
            uh[j] = hi
            ul[j] = lo
            hi_b, lo_b = split(bub[:, j * BLK : (j + 1) * BLK])
            total = total + product3(jnp.concatenate([hi_b, lo_b], axis=0), hi_b, hi, lo, NT)
        part[0, 0] = total[:32]
        part[0, 1] = total[32:]

    def enter():
        pl.semaphore_wait(barrier, len(peers))

    def z_sends(a):
        for i in range(NB):
            z_send(a, i)

    def gram_up_x():
        xu = y_sum(0)
        keep["xu"] = xu
        hi, lo = split(xu)
        cat = jnp.concatenate([hi, lo], axis=0)
        keep["xu_split"] = (hi, cat)
        g = pack(gram(cat))
        gpart[0] = g
        gx[x] = g
        for d in (2, 1, 3):
            copy_to(gpart.at[0], gx.at[x], s_g.at[0], r_g.at[0], to_x(d))

    def second_up():
        hi, cat = keep["xu_split"]
        for i in range(NB):
            j = order[i]
            src[1, j] = product3(cat, hi, uh[j], ul[j], NN)
            x_send(1, i)

    def gram_up_z():
        wait_bytes(gx.at[pl.ds(0, 3)], r_g.at[0])
        g = gx[0] + gx[1] + gx[2] + gx[3]
        gsum[...] = g
        gz[z] = g
        for d in (4, 3, 5, 2, 6, 1, 7):
            copy_to(gsum, gz.at[z], s_g.at[1], r_g.at[1], to_z(lax.rem(z + d, NZ)))

    def second_down():
        prod = jnp.zeros((RANK, BLK), F32)
        gsq = jnp.zeros((RANK, RANK), F32)
        for i in reversed(range(NB)):
            gathered(0, i)
        for j in range(NB):
            hi, lo = split(out[0, j])
            cat = jnp.concatenate([hi, lo], axis=0)
            gsq = gsq + gram(cat)
            prod = prod + product3(cat, hi, dh[j], dl[j], NN)
        g = pack(gsq)
        gpart[1] = g
        gt[t] = g
        part[1, 0] = prod[:32]
        part[1, 1] = prod[32:]
        c_send(1)
        for dy, dc in others_t:
            copy_to(gpart.at[1], gt.at[t], s_g.at[2], r_g.at[2], to_t(dy, dc))

    def factor_up():
        wait_bytes(gz.at[pl.ds(0, 7)], r_g.at[1])
        g = gz[0]
        for s in range(1, NZ):
            g = g + gz[s]
        keep["inv_u"] = triple_left(inverse_factor(unpack(g)))
        left = dot(keep["inv_u"], triple_right(keep["xu"]), NN)
        lu[...] = left
        keep["left_u"] = triple_left(left.T)

    def factor_down():
        wait_bytes(gt.at[pl.ds(0, 7)], r_g.at[2])
        g = gt[0]
        for s in range(1, NY * NC):
            g = g + gt[s]
        keep["inv_d"] = triple_left(inverse_factor(unpack(g)))

    def left_down():
        for j in range(NB):
            left = dot(keep["inv_d"], triple_right(out[0, j]), NN)
            ld[:, j * BLK : (j + 1) * BLK] = left
            lt[j] = triple_left(left.T)

    def last_down():
        right = dot(keep["inv_d"], triple_right(y_sum(1)), NN)
        wd[...] = right
        right = triple_right(right)
        for j in range(NB):
            rd[j * BLK : (j + 1) * BLK, :] = edb[j] - dot(lt[j], right, NN)

    def tensor_sends_done(a):
        wait_bytes(crx.at[a], s_c.at[a])
        wait_bytes(yb.at[a, pl.ds(0, 7)], s_y.at[a])

    enter()
    base_down()
    part_down((0, 1))
    part_up()
    c_send(0)
    part_down((2, 3, 4))
    y_send(0)
    part_down((5, 6))
    z_sends(0)
    gram_up_x()
    second_up()
    reduce_gather(0)
    gram_up_z()
    for i in (6, 5, 4):
        forward(0, i)
    for i in range(4):
        z_send(1, i)
        forward(0, 3 - i)
    for i in (4, 5, 6):
        z_send(1, i)
    factor_up()
    reduce_gather(1)
    second_down()
    for i in (6, 5):
        forward(1, i)
    y_send(1)
    for i in (4, 3, 2, 1, 0):
        forward(1, i)
    factor_down()
    left_down()
    last_down()
    dp_sends_done(0)
    tensor_sends_done(0)
    wait_bytes(gz.at[pl.ds(0, 3)], s_g.at[0])
    wait_bytes(gz.at[pl.ds(0, 7)], s_g.at[1])
    tensor_sends_done(1)
    wait_bytes(gz.at[pl.ds(0, 7)], s_g.at[2])
    inv_out[...] = keep["inv_u"]
    left_out[...] = keep["left_u"]
    for i in reversed(range(NB)):
        gathered(1, i)
    w_out[...] = out[1]
    dp_sends_done(1)


def store_kernel(rd, lu, ld, wd, acc, w, inv, left, o_ru, o_rd, o_lu, o_wu, o_ld, o_wd, ru, wu, sems, sems_u):
    copies = [
        pltpu.make_async_copy(a, b, sems.at[i])
        for i, (a, b) in enumerate(((rd, o_rd), (ld, o_ld), (lu, o_lu), (wd, o_wd)))
    ]
    for copy in copies:
        copy.start()
    rights = [dot(inv[...], triple_right(w[j]), NN) for j in range(NB)]
    for j in range(NB):
        cut = pl.ds(j * BLK, BLK)
        right = rights[j]
        wu[:, cut] = right
        ru[:, cut] = acc[j] - dot(left[...], triple_right(right), NN)
        copy = pltpu.make_async_copy(ru.at[:, cut], o_ru.at[:, cut], sems_u.at[j])
        copy.start()
        copies.append(copy)
    copy = pltpu.make_async_copy(wu, o_wu, sems.at[4])
    copy.start()
    copies.append(copy)
    for copy in copies:
        copy.wait()


def store_all(*arrays):
    wide = NB * BLK
    vmem = pl.BlockSpec(memory_space=pltpu.VMEM)
    dma = pltpu.SemaphoreType.DMA
    return pl.pallas_call(
        store_kernel,
        out_shape=(
            jax.ShapeDtypeStruct((BLK, wide), F32),
            jax.ShapeDtypeStruct((wide, BLK), F32),
            jax.ShapeDtypeStruct((RANK, BLK), F32),
            jax.ShapeDtypeStruct((RANK, wide), F32),
            jax.ShapeDtypeStruct((RANK, wide), F32),
            jax.ShapeDtypeStruct((RANK, BLK), F32),
        ),
        in_specs=[pl.BlockSpec(memory_space=pl.ANY)] * 4 + [vmem] * 4,
        out_specs=(pl.BlockSpec(memory_space=pltpu.HBM),) * 6,
        scratch_shapes=[
            pltpu.VMEM((BLK, wide), F32),
            pltpu.VMEM((RANK, wide), F32),
            dma((5,)),
            dma((NB,)),
        ],
        compiler_params=pltpu.CompilerParams(vmem_limit_bytes=16 * 2**20),
    )(*arrays)


def on_device(up_grad, up_error, up_basis, down_grad, down_error, down_basis):
    arrays = (up_grad, up_error, up_basis.T, down_grad, down_error, down_basis.T)
    hbm = pl.BlockSpec(memory_space=pltpu.HBM)
    vmem = pl.BlockSpec(memory_space=pltpu.VMEM)
    dma = pltpu.SemaphoreType.DMA
    wide = NB * BLK
    results = pl.pallas_call(
        kernel,
        out_shape=(
            pltpu.VMEM((wide, BLK), F32),
            pltpu.VMEM((RANK, BLK), F32),
            pltpu.VMEM((RANK, wide), F32),
            pltpu.VMEM((RANK, BLK), F32),
            pltpu.VMEM((NB, BLK, BLK), F32),
            pltpu.VMEM((NB, RANK, BLK), F32),
            pltpu.VMEM((RANK, 3 * RANK), BF16),
            pltpu.VMEM((BLK, 3 * RANK), BF16),
        ),
        in_specs=[hbm] * 6,
        out_specs=(vmem,) * 8,
        scratch_shapes=[
            pltpu.VMEM((NB, BLK, BLK), BF16),
            pltpu.VMEM((NB, BLK, BLK), BF16),
            pltpu.VMEM((NB, BLK, BLK), BF16),
            pltpu.VMEM((NB, BLK, BLK), BF16),
            pltpu.VMEM((NB, BLK, BLK), F32),
            pltpu.VMEM((NB, BLK, BLK), BF16),
            pltpu.VMEM((NB, BLK, BLK), BF16),
            pltpu.VMEM((RANK, wide), F32),
            pltpu.VMEM((RANK, BLK), F32),
            pltpu.VMEM((2, NB, RANK, BLK), F32),
            pltpu.VMEM((2, NB, 3, SUB, BLK), F32),
            pltpu.VMEM((2, NB, SUB, BLK), F32),
            pltpu.VMEM((2, NZ, SUB, BLK), F32),
            pltpu.VMEM((2, NB, RANK, BLK), F32),
            pltpu.VMEM((2, 2, RANK // 2, BLK), F32),
            pltpu.VMEM((2, RANK // 2, BLK), F32),
            pltpu.VMEM((2, RANK // 2, BLK), F32),
            pltpu.VMEM((2, 8, RANK // 2, BLK), F32),
            pltpu.VMEM((2, RANK // 2, 128), F32),
            pltpu.VMEM((NX, RANK // 2, 128), F32),
            pltpu.VMEM((NZ, RANK // 2, 128), F32),
            pltpu.VMEM((RANK // 2, 128), F32),
            pltpu.VMEM((NY * NC, RANK // 2, 128), F32),
            pltpu.VMEM((NB, BLK, 3 * RANK), BF16),
            dma((4, NB)),
            dma((2,)),
            dma((2,)),
            dma((2,)),
            dma((2,)),
            dma((2, NB)),
            dma((2,)),
            dma((2, NB)),
            dma((2, NB)),
            dma((2,)),
            dma((2,)),
            dma((2,)),
            dma((2,)),
            dma((3,)),
            dma((3,)),
        ],
        compiler_params=pltpu.CompilerParams(
            collective_id=0, has_side_effects=True, vmem_limit_bytes=32 * 2**20
        ),
    )(*(pltpu.with_memory_space_constraint(a, pltpu.HBM) for a in arrays))
    ru, rd, lu, wu, ld, wd = store_all(*results)
    return ru, rd, lu.T, wu.T, ld.T, wd.T


def solution(mesh):
    placed = (
        P("dp", "tensor"),
        P("dp", "tensor"),
        P("tensor", None),
        P("tensor", "dp"),
        P("tensor", "dp"),
        P("dp", None),
    )
    return jax.shard_map(
        on_device,
        mesh=mesh,
        in_specs=placed,
        out_specs=(
            P("dp", "tensor"),
            P("tensor", "dp"),
            P("dp", None),
            P("tensor", None),
            P("tensor", None),
            P("dp", None),
        ),
        check_vma=False,
    )
```
